128 devices in a mesh: grp: 8 (over x_lo, z), vocab: 16 (over x_hi, y, core).
Axes of the slice: x: 4 (x_hi: 2, x_lo: 2; x = x_hi * 2 + x_lo), y: 4, z: 4, core: 2. Of those that a mesh axis runs over, the one named last changes fastest.
Arguments:
- teacher_hidden: bfloat16 [512, 4096], P('grp', 'vocab'), may hold values from -120 to 120
- student_hidden: bfloat16 [512, 5120], P('grp', 'vocab'), may hold values from -120 to 120
- teacher_head: bfloat16 [4096, 81920], P(None, ('grp', 'vocab')), may hold values from -0.09375 to 0.09375
- student_head: bfloat16 [5120, 81920], P(None, ('grp', 'vocab')), may hold values from -0.078125 to 0.078125
- lengths: int32 [8], replicated, may hold values from 1 to 128, 512 in all
- sampled: int32 [512], P('grp'), may hold values from 0 to 81919
Outputs:
- head_grad: bfloat16 [5120, 81920], P(None, ('grp', 'vocab'))
- hidden_grad: bfloat16 [512, 5120], P('grp', 'vocab')
- token_kl: float32 [512], P(('grp', 'vocab'))
- sample_ratio: float32 [512], P(('grp', 'vocab'))
The draws below stay inside these ranges and needn't reach their ends.
Inputs may be any that keep to these rules, and one draw needn't show every extreme that they name: The lengths sum to 512; the longest is exactly 128.
All inputs are finite; a program needn't handle non-finite values.
Results may differ from the reference program's by a relative error of at most 0.0065.
Values may be sent and summed in bfloat16 or wider, within the bound.
No kernel may reach another device: no remote copies, remote signals or barrier semaphores. Data moves between devices by JAX's collectives and lax.ppermute only.
A program may use at most 128 MiB of HBM per device.

```python
import math
import jax
import jax.numpy as jnp
import numpy as np

DT = 4096
DS = 5120
VOCAB = 81920
NSEQ = 8
LOSS_SCALE = 16
TOKENS = 512
MAXLEN = 128


def drawn_rows(key, width):
    values = jax.random.normal(key, (TOKENS, width), jnp.float32)
    return jnp.clip(3.0 * values, -24.0, 24.0)


def draw_teacher_hidden(key, part):
    key = jax.random.fold_in(key, 11)
    return drawn_rows(key, DT).astype(jnp.bfloat16)


def draw_student_hidden(key, part):
    key = jax.random.fold_in(key, 23)
    return drawn_rows(key, DS).astype(jnp.bfloat16)


def plant(drawn, stream_key, least, largest):
    longest = drawn.shape.index(max(drawn.shape))
    spots = []
    for shift in (0, 1):
        where = [jax.random.randint(jax.random.fold_in(stream_key, axis), (), 0, length) for axis, length in enumerate(drawn.shape)]
        where[longest] = (where[longest] + shift) % drawn.shape[longest]
        spots.append(tuple(where))
    return drawn.at[spots[0]].set(least).at[spots[1]].set(largest)


def level_of(rng, dims, cuts, least, high):
    factor_of, own = 1.0, jax.random.fold_in(rng, 6)
    for axis_at, parts in cuts:
        steps = jnp.exp(jax.random.uniform(jax.random.fold_in(own, axis_at), (parts,), jnp.float32, least / len(cuts), high / len(cuts)))
        factor_of = factor_of * jnp.repeat(steps, dims[axis_at] // parts).reshape([-1 if axis == axis_at else 1 for axis in range(len(dims))])
    return factor_of


def skewed_wide(key, shape, amount, lean):
    weights = [min(1 << octave, amount + 1 - (1 << octave)) * (1 << 20) // math.isqrt((1 << octave) ** lean) + 1 for octave in range((amount + 1).bit_length()) if 1 << octave <= amount]
    scale = 1 + sum(weights) // (1 << 30)
    listing = np.cumsum(np.array([max(1, weight // scale) for weight in weights]))
    pick = jax.random.randint(jax.random.fold_in(key, 1), shape, 0, int(listing[len(weights) - 1]))
    start = jnp.left_shift(1, jnp.searchsorted(jnp.asarray(listing, jnp.int32), pick, side="right").astype(jnp.int32))
    grade = start - 1 + jax.random.randint(jax.random.fold_in(key, 4), shape, 0, 1 << 30) % jnp.minimum(start, amount + 1 - start)
    return jax.random.permutation(jax.random.fold_in(key, 2), amount)[grade].astype(jnp.int32)


def profile(number_of, total, most, lean):
    weights = [(1 << 20) // math.isqrt(rank ** lean) + 1 for rank in range(2, number_of + 1)]
    spare, holding = total - most - (number_of - 1), [1] * (number_of - 1)
    while spare > 0:
        free = [i for i in range(number_of - 1) if holding[i] < most]
        mass, remaining = sum([weights[i] for i in free]), spare
        for i in free:
            extra = min(most - holding[i], max(1, remaining * weights[i] // mass), spare)
            holding[i] = holding[i] + extra
            spare = spare - extra
    return np.array([most] + holding)


def ragged_sizes(rng, count, total, bound, slope):
    if count == 2:
        one = jax.random.randint(rng, (), max(1, total - bound), min(bound, total - 1) + 1)
        return jnp.stack([one, total - one])
    tallies = jnp.asarray(profile(count, total, bound, slope), jnp.int32)
    twos = (count - 1) // 2
    giver, taker = tallies[1:1 + 2 * twos:2], tallies[2:2 + 2 * twos:2]
    slack = jnp.minimum(giver - 1, bound - taker)
    shifted = jax.random.randint(jax.random.fold_in(rng, 1), (twos,), 0, 1 << 20) % (slack + 1)
    tallies = tallies.at[1:1 + 2 * twos:2].set(giver - shifted).at[2:2 + 2 * twos:2].set(taker + shifted)
    return tallies[jax.random.permutation(jax.random.fold_in(rng, 2), count)]


def centred(own_key, extent, deviation, bound, pieces=(), held_as=jnp.bfloat16):
    result = deviation * jax.random.normal(own_key, extent, jnp.float32)
    if pieces:
        result = result * level_of(own_key, extent, pieces, -0.22, 0.18)
    return jnp.clip(result, -bound, bound).astype(held_as)


def setup_inputs(seed: int = 0) -> dict:
    seeds = jax.random.split(jax.random.key(seed), 7)
    return {
        "teacher_hidden": draw_teacher_hidden(jax.random.fold_in(seeds[6], 71), 0),
        "student_hidden": draw_student_hidden(jax.random.fold_in(seeds[6], 71), 0),
        "teacher_head": centred(seeds[2], (DT, VOCAB), DT ** -0.5, 0.09375, ((1, 128),)),
        "student_head": centred(seeds[3], (DS, VOCAB), DS ** -0.5, 0.078125, ((1, 128),)),
        "lengths": ragged_sizes(seeds[4], NSEQ, TOKENS, MAXLEN, 2).astype(jnp.int32),
        "sampled": plant(skewed_wide(seeds[5], (TOKENS,), VOCAB, 2), jax.random.fold_in(seeds[5], 3), 0, VOCAB - 1).astype(jnp.int32),
    }


def reference(teacher_hidden, student_hidden, teacher_head, student_head, lengths, sampled):
    teacher_logits = jnp.dot(teacher_hidden, teacher_head, preferred_element_type=jnp.float32)
    student_logits = jnp.dot(student_hidden, student_head, preferred_element_type=jnp.float32)
    teacher_logp = teacher_logits - jax.nn.logsumexp(teacher_logits, axis=1, keepdims=True)
    student_logp = student_logits - jax.nn.logsumexp(student_logits, axis=1, keepdims=True)
    teacher_prob = jnp.exp(teacher_logp)
    student_prob = jnp.exp(student_logp)
    log_ratio = teacher_logp - student_logp
    token_kl = jnp.sum(teacher_prob * log_ratio, axis=1)
    sample_ratio = jnp.take_along_axis(log_ratio, sampled.astype(jnp.int32)[:, None], axis=1)[:, 0]
    ends = jnp.cumsum(lengths).astype(jnp.int32)
    starts = (ends - lengths).astype(jnp.int32)
    position = jnp.arange(TOKENS, dtype=jnp.int32)[:, None]
    inside = (position >= starts[None, :]) & (position < ends[None, :])
    seq_len = jnp.sum(jnp.where(inside, lengths[None, :], 0), axis=1)
    weight = (LOSS_SCALE * TOKENS / NSEQ) / seq_len.astype(jnp.float32)
    logit_grad = (weight[:, None] * (student_prob - teacher_prob)).astype(jnp.bfloat16)
    head_grad = jnp.dot(student_hidden.T, logit_grad, preferred_element_type=jnp.float32).astype(jnp.bfloat16)
    hidden_grad = jnp.dot(logit_grad, student_head.T, preferred_element_type=jnp.float32).astype(jnp.bfloat16)
    return head_grad, hidden_grad, token_kl, sample_ratio
```

```python
import itertools

import jax
import jax.numpy as jnp
import numpy as np
from jax import lax
from jax.experimental import pallas as pl
from jax.experimental.pallas import tpu as pltpu
from jax.sharding import PartitionSpec as P

LOSS_SCALE = 16
BOTH = ("grp", "vocab")
F32, BF16 = jnp.float32, jnp.bfloat16
HALF = 32
LANES = 128
ID_ROWS = 16


def device(x, y, z, core):
    return ((x % 2) * 4 + z) * 16 + ((x // 2) * 4 + y) * 2 + core


def cubes(core, step, rank):
    seen, groups = set(), []
    for where in itertools.product(range(4), repeat=3):
        if where in seen:
            continue
        pairs = [sorted((p, p ^ step), key=rank) for p in where]
        members = list(itertools.product(*pairs))
        seen.update(members)
        groups.append([device(*m, core) for m in members])
    return groups


def low(p):
    return p & 1


def high(p):
    return p >> 1


def parity(p):
    return (p & 1) ^ (p >> 1)


FIRST = cubes(0, 1, low) + cubes(1, 3, high)
SECOND = cubes(0, 3, high) + cubes(1, 1, parity)
SAME_CORE = [[2 * chip + core for chip in range(64)] for core in (0, 1)]
SWAP = [(i, i ^ 1) for i in range(128)]


def positions():
    table = np.zeros((2, 64), np.int32)
    for x, y, z in itertools.product(range(4), repeat=3):
        chip = ((x % 2) * 4 + z) * 8 + (x // 2) * 4 + y

        def number(rank):
            return rank(x) * 4 + rank(y) * 2 + rank(z)

        table[0, chip] = number(high) * 8 + number(low)
        table[1, chip] = number(parity) * 8 + number(high)
    return table


POSITIONS = positions()


def swap(value):
    return lax.ppermute(value, BOTH, SWAP)


def to_all(block, groups):
    size = len(groups[0])
    return lax.all_to_all(
        jnp.broadcast_to(block, (size,) + block.shape), BOTH, 0, 0, axis_index_groups=groups
    )


def rows_of(table_ref, blocks_ref, chunk, strips):
    parts = [blocks_ref[table_ref[group * 8 + chunk]] for group in range(8)]
    return jnp.concatenate(
        [
            jnp.concatenate([p[s * HALF : (s + 1) * HALF] for p in parts], axis=0)
            for s in range(strips)
        ],
        axis=1,
    )


def add_up(k, out_ref, term):
    @pl.when(k == 0)
    def _():
        out_ref[...] = term

    @pl.when(k > 0)
    def _():
        out_ref[...] += term


def teacher_kernel(table_ref, blocks_ref, own_ref, other_ref, out_ref):
    k = pl.program_id(0)
    lhs = rows_of(table_ref, blocks_ref, k, 4)
    rhs = jnp.concatenate([own_ref[...], other_ref[...]], axis=1)
    add_up(k, out_ref, jnp.dot(lhs, rhs, preferred_element_type=F32))


def student_kernel(
    table_ref, first_ref, blocks_ref, own_ref, other_ref, teacher_ref, ids_ref, out_ref, stats_ref, work
):
    k = pl.program_id(0)
    lhs = rows_of(table_ref, blocks_ref, k, 5)
    rhs = jnp.concatenate([own_ref[...], other_ref[...]], axis=1)
    add_up(k, out_ref, jnp.dot(lhs, rhs, preferred_element_type=F32))

    @pl.when(k == 7)
    def _():
        columns = own_ref.shape[1]
        step = 16
        lane = lax.broadcasted_iota(jnp.int32, (step, LANES), 1)
        column = lax.broadcasted_iota(jnp.int32, (step, columns), 1)
        column = jnp.concatenate([column + first_ref[0], column + first_ref[1]], axis=1)

        def body(i, carry):
            rows = pl.ds(pl.multiple_of(i * step, step), step)
            t, s = teacher_ref[rows, :], out_ref[rows, :]
            top_t = jnp.max(t, axis=1, keepdims=True)
            top_s = jnp.max(s, axis=1, keepdims=True)
            picked = jnp.sum(jnp.where(column == ids_ref[rows, :], t - s, 0.0), axis=1, keepdims=True)
            t, s = t - top_t, s - top_s
            e = jnp.exp(t)
            sum_t = jnp.sum(e, axis=1, keepdims=True)
            sum_s = jnp.sum(jnp.exp(s), axis=1, keepdims=True)
            term = jnp.sum(e * (t - s), axis=1, keepdims=True)
            row = jnp.zeros((step, LANES), F32)
            for j, value in enumerate((top_t, sum_t, top_s, sum_s, term, picked)):
                row = jnp.where(lane == j, value, row)
            work[rows, :] = row
            return carry

        lax.fori_loop(0, out_ref.shape[0] // step, body, 0)
        stats = work[...].T[:8, :]
        stats_ref[...] = jnp.broadcast_to(stats, stats_ref.shape)


def gradient_kernel(
    stats_ref, weight_ref, teacher_ref, student_ref, own_ref, other_ref, part_ref, mine_ref, theirs_ref, kl_ref, work
):
    k = pl.program_id(0)
    columns = own_ref.shape[1]

    @pl.when(k == 0)
    def _():
        top_t, sum_t, top_s, sum_s, term, picked = (stats_ref[:, j, :] for j in range(6))
        whole_t = jnp.max(top_t, axis=0, keepdims=True)
        whole_s = jnp.max(top_s, axis=0, keepdims=True)
        scale_t = jnp.exp(top_t - whole_t)
        total_t = jnp.sum(scale_t * sum_t, axis=0, keepdims=True)
        total_s = jnp.sum(jnp.exp(top_s - whole_s) * sum_s, axis=0, keepdims=True)
        log_t, log_s = jnp.log(total_t), jnp.log(total_s)
        shift = (top_t - whole_t) - (top_s - whole_s)
        kl = jnp.sum(scale_t * (term + sum_t * shift), axis=0, keepdims=True) / total_t - (log_t - log_s)
        lse_t, lse_s = whole_t + log_t, whole_s + log_s
        ratio = jnp.sum(picked, axis=0, keepdims=True) - (lse_t - lse_s)
        tokens = kl.shape[1]
        kl_ref[...] = jnp.concatenate([kl, ratio, jnp.zeros((6, tokens), F32)], axis=0)
        rows = jnp.concatenate(
            [lse_t, lse_s, weight_ref[...], jnp.zeros((LANES - 3, tokens), F32)], axis=0
        )
        work[...] = rows.T
        step = 16

        def body(i, carry):
            at = pl.ds(pl.multiple_of(i * step, step), step)
            at_t, at_s, weight = (work[at, j : j + 1] for j in range(3))
            grad = weight * (jnp.exp(student_ref[at, :] - at_s) - jnp.exp(teacher_ref[at, :] - at_t))
            grad = grad.astype(BF16)
            mine_ref[at, :] = grad[:, :columns]
            theirs_ref[at, :] = grad[:, columns:]
            return carry

        lax.fori_loop(0, tokens // step, body, 0)

    grad = jnp.concatenate([mine_ref[...], theirs_ref[...]], axis=1)
    head = jnp.concatenate([own_ref[...], other_ref[...]], axis=1)
    part = lax.dot_general(grad, head, (((1,), (1,)), ((), ())), preferred_element_type=F32).astype(BF16)
    width = part_ref.shape[3]
    for group in range(8):
        for j in range(part_ref.shape[1]):
            part_ref[group, j] = part[group * HALF : (group + 1) * HALF, j * width : (j + 1) * width]


def head_kernel(table_ref, other_table_ref, blocks_ref, other_blocks_ref, mine_ref, got_ref, out_ref):
    k = pl.program_id(0)
    rows = jnp.concatenate(
        [rows_of(table_ref, blocks_ref, k, 5), rows_of(other_table_ref, other_blocks_ref, k, 5)], axis=0
    )
    grad = jnp.concatenate([mine_ref[...], got_ref[...]], axis=0)
    out_ref[...] = lax.dot_general(
        rows, grad, (((0,), (0,)), ((), ())), preferred_element_type=F32
    ).astype(BF16)


def whole(shape):
    return pl.BlockSpec(shape, lambda k, *_: (0,) * len(shape))


def call(kernel, name, scalars, grid, in_specs, out_specs, out_shape, flops, size, scratch=(), limit=40):
    return pl.pallas_call(
        kernel,
        name=name,
        grid_spec=pltpu.PrefetchScalarGridSpec(
            num_scalar_prefetch=scalars,
            grid=(grid,),
            in_specs=in_specs,
            out_specs=out_specs,
            scratch_shapes=list(scratch),
        ),
        out_shape=out_shape,
        compiler_params=pltpu.CompilerParams(vmem_limit_bytes=limit << 20),
        cost_estimate=pl.CostEstimate(flops=flops, bytes_accessed=size, transcendentals=0),
    )


def weights(lengths, total_rows):
    seq_count = lengths.shape[0]
    ends = jnp.cumsum(lengths)
    starts = ends - lengths
    position = jnp.arange(total_rows, dtype=jnp.int32)[:, None]
    inside = (position >= starts[None, :]) & (position < ends[None, :])
    seq_len = jnp.sum(jnp.where(inside, lengths[None, :], 0), axis=1)
    return LOSS_SCALE * total_rows / seq_count / seq_len.astype(F32)


def per_device(teacher_hidden, student_hidden, teacher_head, student_head, lengths, sampled):
    group, member = lax.axis_index("grp"), lax.axis_index("vocab")
    core = member % 2
    is_first = core == 0
    wide_t, columns = teacher_head.shape
    wide_s = student_head.shape[0]
    tokens = 8 * HALF
    part_t, part_s = wide_t // 8, wide_s // 8
    strips_t, strips_s = part_t // LANES, part_s // LANES

    both = jnp.concatenate([teacher_hidden, student_hidden], axis=1).reshape(2, HALF, -1)
    mine = jnp.where(is_first, both[0], both[1])
    got = swap(jnp.where(is_first, both[1], both[0]))
    left, right = jnp.where(is_first, mine, got), jnp.where(is_first, got, mine)
    cut = part_t // 2

    def strips(a, b, count):
        rows = jnp.concatenate([a, b], axis=1).reshape(HALF, count, LANES)
        return rows.transpose(1, 0, 2).reshape(count * HALF, LANES)

    ids = sampled.reshape(2, HALF)
    ids = jnp.where(is_first, ids[0], ids[1])
    digits = jnp.stack([ids // 4096, (ids // 64) % 64, ids % 64]).astype(BF16)
    digits = jnp.pad(digits, ((0, ID_ROWS - 3), (0, LANES - HALF)))
    block = jnp.concatenate(
        [
            strips(left[:, :cut], right[:, :cut], strips_t),
            digits,
            strips(left[:, cut:], right[:, cut:], strips_s),
        ]
    )
    rows_t = strips_t * HALF + ID_ROWS
    near = to_all(block, FIRST)
    other_teacher_head = swap(teacher_head)
    other_student_head = swap(student_head)
    teacher_blocks = to_all(near[:, :rows_t], SECOND).reshape(64, rows_t, LANES)
    student_blocks = to_all(near[:, rows_t:], SECOND).reshape(64, strips_s * HALF, LANES)

    tables = jnp.asarray(POSITIONS)
    table = jnp.where(is_first, tables[0], tables[1])
    other_table = jnp.where(is_first, tables[1], tables[0])
    digits = teacher_blocks[:, rows_t - ID_ROWS : rows_t - ID_ROWS + 3, :HALF].astype(jnp.int32)
    digits = digits[table.reshape(8, 8)[:, 0]]
    all_ids = (digits[:, 0] * 4096 + digits[:, 1] * 64 + digits[:, 2]).reshape(tokens, 1)

    number = group * lax.axis_size("vocab") + member
    first = jnp.stack([number * columns, (number + 1 - 2 * core) * columns]).astype(jnp.int32)
    logits = jax.ShapeDtypeStruct((tokens, 2 * columns), F32)
    teacher_logits = call(
        teacher_kernel,
        "teacher_logits",
        1,
        8,
        [
            whole((64, rows_t, LANES)),
            pl.BlockSpec((part_t, columns), lambda k, *_: (k, 0)),
            pl.BlockSpec((part_t, columns), lambda k, *_: (k, 0)),
        ],
        whole((tokens, 2 * columns)),
        logits,
        4 * tokens * wide_t * columns,
        4 * wide_t * columns,
    )(table, teacher_blocks, teacher_head, other_teacher_head)
    student_logits, stats = call(
        student_kernel,
        "student_logits",
        2,
        8,
        [
            whole((64, strips_s * HALF, LANES)),
            pl.BlockSpec((part_s, columns), lambda k, *_: (k, 0)),
            pl.BlockSpec((part_s, columns), lambda k, *_: (k, 0)),
            whole((tokens, 2 * columns)),
            whole((tokens, 1)),
        ],
        [whole((tokens, 2 * columns)), whole((64, 8, tokens))],
        [logits, jax.ShapeDtypeStruct((64, 8, tokens), F32)],
        4 * tokens * wide_s * columns,
        4 * wide_s * columns,
        scratch=[pltpu.VMEM((tokens, LANES), F32)],
    )(table, first, student_blocks, student_head, other_student_head, teacher_logits, all_ids)
    all_stats = lax.all_to_all(stats, BOTH, 0, 0, axis_index_groups=SAME_CORE)

    weight = weights(lengths, 2 * tokens).reshape(8, 2, HALF)
    weight = jnp.where(is_first, weight[:, 0], weight[:, 1]).reshape(1, tokens)
    grads = jax.ShapeDtypeStruct((tokens, columns), BF16)
    part, mine_grad, their_grad, kl = call(
        gradient_kernel,
        "hidden_gradient",
        0,
        4,
        [
            whole((64, 8, tokens)),
            whole((1, tokens)),
            whole((tokens, 2 * columns)),
            whole((tokens, 2 * columns)),
            pl.BlockSpec((2 * part_s, columns), lambda k: (k, 0)),
            pl.BlockSpec((2 * part_s, columns), lambda k: (k, 0)),
        ],
        [
            pl.BlockSpec((8, 2, HALF, part_s), lambda k: (0, k, 0, 0)),
            whole((tokens, columns)),
            whole((tokens, columns)),
            whole((8, tokens)),
        ],
        [
            jax.ShapeDtypeStruct((8, 8, HALF, part_s), BF16),
            grads,
            grads,
            jax.ShapeDtypeStruct((8, tokens), F32),
        ],
        4 * tokens * wide_s * columns,
        4 * wide_s * columns,
        scratch=[pltpu.VMEM((tokens, LANES), F32)],
    )(all_stats, weight, teacher_logits, student_logits, student_head, other_student_head)

    parts = lax.all_to_all(part.reshape(64, HALF, part_s), BOTH, 0, 0, axis_index_groups=SAME_CORE)
    hidden = jnp.sum(parts.astype(F32), axis=0).astype(BF16)
    one, two = hidden[:, : part_s // 2], hidden[:, part_s // 2 :]
    kept = jnp.where(is_first, one, two)
    got = swap(jnp.where(is_first, two, one))
    hidden_grad = jnp.concatenate(
        [jnp.where(is_first, kept, got), jnp.where(is_first, got, kept)], axis=0
    )

    other_blocks = swap(student_blocks)
    got_grad = swap(their_grad)
    head_grad = call(
        head_kernel,
        "head_gradient",
        2,
        8,
        [
            whole((64, strips_s * HALF, LANES)),
            whole((64, strips_s * HALF, LANES)),
            whole((tokens, columns)),
            whole((tokens, columns)),
        ],
        pl.BlockSpec((part_s, columns), lambda k, *_: (k, 0)),
        jax.ShapeDtypeStruct((wide_s, columns), BF16),
        4 * tokens * wide_s * columns,
        4 * wide_s * columns,
    )(table, other_table, student_blocks, other_blocks, mine_grad, got_grad)

    def own_tokens(who):
        return lax.dynamic_slice(kl, (0, group * HALF + (4 * who) % HALF), (2, 4))

    got = swap(own_tokens(member + 1 - 2 * core))
    out = jnp.where(member // 8 == core, own_tokens(member), got)
    return head_grad, hidden_grad, out[0], out[1]


def solution(mesh):
    return jax.shard_map(
        per_device,
        mesh=mesh,
        in_specs=(
            P("grp", "vocab"),
            P("grp", "vocab"),
            P(None, BOTH),
            P(None, BOTH),
            P(),
            P("grp"),
        ),
        out_specs=(P(None, BOTH), P("grp", "vocab"), P(BOTH), P(BOTH)),
        check_vma=False,
    )
```

```python
import functools
import itertools

import jax
import jax.numpy as jnp
import numpy as np
from jax import lax
from jax.experimental import pallas as pl
from jax.experimental.pallas import tpu as pltpu
from jax.sharding import PartitionSpec as P

LOSS_SCALE = 16
BOTH = ("grp", "vocab")
F32, BF16 = jnp.float32, jnp.bfloat16
HALF = 32
LANES = 128
ID_ROWS = 16
PIECES = 2
LIMIT = 56
DEPTH = 4
CORNER_OF = (0, 4, 2, 1, 3, 5, 6, 7)


def device(x, y, z, core):
    return ((x % 2) * 4 + z) * 16 + ((x // 2) * 4 + y) * 2 + core


def cubes(core, step, rank):
    seen, groups = set(), []
    for where in itertools.product(range(4), repeat=3):
        if where in seen:
            continue
        pairs = [sorted((p, p ^ step), key=rank) for p in where]
        members = list(itertools.product(*pairs))
        seen.update(members)
        groups.append([device(*m, core) for m in members])
    return groups


def low(p):
    return p & 1


def high(p):
    return p >> 1


def parity(p):
    return (p & 1) ^ (p >> 1)


FIRST = cubes(0, 1, low) + cubes(1, 3, high)
SAME_CORE = [[2 * chip + core for chip in range(64)] for core in (0, 1)]
SWAP = [(i, i ^ 1) for i in range(128)]


def chips():
    return itertools.product(range(4), repeat=3)


def number(rank, place):
    return rank(place[0]) * 4 + rank(place[1]) * 2 + rank(place[2])


def positions():
    table = np.zeros((2, 64), np.int32)
    for place in chips():
        chip = device(*place, 0) // 2
        table[0, chip] = number(high, place) * 8 + number(low, place)
        table[1, chip] = number(parity, place) * 8 + number(high, place)
    return table


def corners():
    table = np.zeros(128, np.int32)
    for place in chips():
        table[device(*place, 0)] = number(high, place)
        table[device(*place, 1)] = number(parity, place)
    return table


def links(axes):
    pairs = []
    for place in chips():
        for core in (0, 1):
            other = list(place)
            for axis in axes:
                other[axis] ^= (3, 1)[core]
            pairs.append((device(*place, core), device(*other, core)))
    return pairs


POSITIONS = positions()
CORNERS = corners()


def swap(value):
    return lax.ppermute(value, BOTH, SWAP)


def to_all(block, groups):
    size = len(groups[0])
    return lax.all_to_all(
        jnp.broadcast_to(block, (size,) + block.shape), BOTH, 0, 0, axis_index_groups=groups
    )


def second_gather(near):
    def along(value, *axes):
        return lax.ppermute(value, BOTH, links(axes))

    one = [along(near, axis) for axis in range(3)]
    far = along(near, 0, 1, 2)
    two = [along(one[(axis + 2) % 3], (axis + 1) % 3) for axis in range(3)]
    return [near, *one, *two, far]


def rows_of(table_ref, blocks_ref, chunk, at, strips):
    parts = [blocks_ref[table_ref[group * 8 + chunk], at : at + strips * HALF] for group in range(8)]
    return jnp.concatenate(
        [
            jnp.concatenate([p[s * HALF : (s + 1) * HALF] for p in parts], axis=0)
            for s in range(strips)
        ],
        axis=1,
    )


class Stream:
    def __init__(self, sems):
        self.sems = sems
        self.copies = []
        self.started = 0

    def add(self, source, target):
        self.copies.append(pltpu.make_async_copy(source, target, self.sems.at[len(self.copies)]))
        return len(self.copies) - 1

    def start(self, count):
        for copy in self.copies[self.started : count]:
            copy.start()
        self.started = max(self.started, min(count, len(self.copies)))

    def wait(self, i):
        self.copies[i].wait()
        self.start(i + 1 + DEPTH)


def put_beside(pairs_and_buffers, sems):
    copies = []
    for pair, buffer in pairs_and_buffers:
        rows, columns = pair[0].shape
        size = rows // 4
        for i in range(4):
            for j, ref in enumerate(pair):
                at = pl.ds(i * size, size)
                copies.append(
                    pltpu.make_async_copy(
                        ref.at[at], buffer.at[at, pl.ds(j * columns, columns)], sems.at[len(copies)]
                    )
                )
                copies[-1].start()
    for copy in copies:
        copy.wait()


def prefetch_kernel(own_t, other_t, own_s, other_s, first, second, third, heads_t, heads_s, sems):
    put_beside([((own_t, other_t), heads_t), ((own_s, other_s), heads_s)], sems)


def logits_kernel(
    table_ref, place_ref, *refs
):
    units, (heads_t, heads_s, teacher, student, stats_out, lhs_out) = refs[:8], refs[8:14]
    blocks_ref, lhs_t, lhs_s, powers, stats, work, sems, out_sems = refs[14:]
    arriving = []
    for n, unit in enumerate(units):
        start = (place_ref[2] ^ CORNER_OF[n]) * 8
        arriving.append(pltpu.make_async_copy(unit, blocks_ref.at[pl.ds(start, 8)], sems.at[n]))
        arriving[-1].start()
    columns = heads_t.shape[1] // 2
    lane = lax.broadcasted_iota(jnp.int32, (HALF, LANES), 1)
    column = lax.broadcasted_iota(jnp.int32, (HALF, columns), 1)
    column = jnp.concatenate([column + place_ref[0], column + place_ref[1]], axis=1)
    at_s = 4 * HALF + ID_ROWS

    def columns_of(values, first):
        row = jnp.zeros((HALF, LANES), F32)
        for j, value in enumerate(values):
            row = jnp.where(lane == first + j, value, row)
        return row

    for copy in arriving:
        copy.wait()
    for chunk in range(8):
        lhs_t[:, chunk * 4 * LANES : (chunk + 1) * 4 * LANES] = rows_of(table_ref, blocks_ref, chunk, 0, 4)
    teacher[...] = jnp.dot(lhs_t[...], heads_t[...], preferred_element_type=F32)
    for chunk in range(8):
        lhs_s[:, chunk * 5 * LANES : (chunk + 1) * 5 * LANES] = rows_of(table_ref, blocks_ref, chunk, at_s, 5)
    leaving = [pltpu.make_async_copy(lhs_s, lhs_out, out_sems.at[0])]
    leaving[0].start()
    digits = [blocks_ref[table_ref[group * 8], 4 * HALF : at_s].astype(F32) for group in range(8)]
    ids = jnp.concatenate([d[0:1] * 4096.0 + d[1:2] * 64.0 + d[2:3] for d in digits], axis=0)
    ids = jnp.concatenate([ids, jnp.zeros((LANES - 8, LANES), F32)], axis=0).T.astype(jnp.int32)
    for group in range(8):
        rows = pl.ds(group * HALF, HALF)
        t = teacher[rows, :]
        top = jnp.max(t, axis=1, keepdims=True)
        t = t - top
        e = jnp.exp(t)
        powers[rows, :] = e
        work[rows, :] = columns_of(
            (top, jnp.sum(e, axis=1, keepdims=True), jnp.sum(e * t, axis=1, keepdims=True)), 0
        )
    student[...] = jnp.dot(lhs_s[...], heads_s[...], preferred_element_type=F32)
    for group in range(8):
        rows = pl.ds(group * HALF, HALF)
        s = student[rows, :]
        hit = column == ids[:HALF, group : group + 1]
        picked = jnp.sum(jnp.where(hit, teacher[rows, :] - s, 0.0), axis=1, keepdims=True)
        top = jnp.max(s, axis=1, keepdims=True)
        s = s - top
        total = jnp.sum(jnp.exp(s), axis=1, keepdims=True)
        term = jnp.sum(powers[rows, :] * s, axis=1, keepdims=True)
        work[rows, :] += columns_of((top, total, term, picked), 3)
    stats[...] = jnp.broadcast_to(work[...].T[:8, :], stats.shape)
    leaving.append(pltpu.make_async_copy(stats, stats_out, out_sems.at[1]))
    leaving[1].start()
    for copy in leaving:
        copy.wait()


def gradient_kernel(
    stats_ref, weight_ref, teacher, student, own_s, other_s, part_out, grads_out, kl_ref,
    heads, part, grads, work, sems, out_sems,
):
    stream = Stream(sems)
    size, columns = own_s.shape[0] // 4, own_s.shape[1]
    for i in range(4):
        at = pl.ds(i * size, size)
        for j, ref in enumerate((own_s, other_s)):
            stream.add(ref.at[at], heads.at[at, pl.ds(j * columns, columns)])
    stream.start(DEPTH)
    top_t, sum_t, term_t, top_s, sum_s, term_s, picked = (stats_ref[:, j, :] for j in range(7))
    whole_t = jnp.max(top_t, axis=0, keepdims=True)
    whole_s = jnp.max(top_s, axis=0, keepdims=True)
    scale_t = jnp.exp(top_t - whole_t)
    total_t = jnp.sum(scale_t * sum_t, axis=0, keepdims=True)
    total_s = jnp.sum(jnp.exp(top_s - whole_s) * sum_s, axis=0, keepdims=True)
    log_t, log_s = jnp.log(total_t), jnp.log(total_s)
    shift = (top_t - whole_t) - (top_s - whole_s)
    kl = jnp.sum(scale_t * (term_t - term_s + sum_t * shift), axis=0, keepdims=True) / total_t - (log_t - log_s)
    lse_t, lse_s = whole_t + log_t, whole_s + log_s
    ratio = jnp.sum(picked, axis=0, keepdims=True) - (lse_t - lse_s)
    tokens = kl.shape[1]
    kl_ref[...] = jnp.concatenate([kl, ratio, jnp.zeros((6, tokens), F32)], axis=0)
    rows = jnp.concatenate([lse_t, lse_s, weight_ref[...], jnp.zeros((LANES - 3, tokens), F32)], axis=0)
    work[...] = rows.T

    for i in range(tokens // HALF):
        at = pl.ds(i * HALF, HALF)
        at_t, at_s, weight = (work[at, j : j + 1] for j in range(3))
        grad = weight * (jnp.exp(student[at, :] - at_s) - jnp.exp(teacher[at, :] - at_t))
        grads[at, :] = grad.astype(BF16)
    leaving = [pltpu.make_async_copy(grads, grads_out, out_sems.at[4])]
    leaving[0].start()
    width = part.shape[3]
    chunks = size // width
    for i in range(4):
        stream.wait(2 * i)
        stream.wait(2 * i + 1)
        product = lax.dot_general(
            grads[...], heads[i * size : (i + 1) * size, :], (((1,), (1,)), ((), ())), preferred_element_type=F32
        ).astype(BF16)
        for group in range(8):
            for j in range(chunks):
                part[group, chunks * i + j] = product[
                    group * HALF : (group + 1) * HALF, j * width : (j + 1) * width
                ]
        at = pl.ds(chunks * i, chunks)
        leaving.append(pltpu.make_async_copy(part.at[:, at], part_out.at[:, at], out_sems.at[i]))
        leaving[-1].start()
    for copy in leaving:
        copy.wait()


def head_kernel(own_ref, other_ref, mine_ref, got_ref, out_ref):
    rows = jnp.concatenate([own_ref[...], other_ref[...]], axis=0)
    grad = jnp.concatenate([mine_ref[...], got_ref[...]], axis=0)
    out_ref[...] = lax.dot_general(
        rows, grad, (((0,), (0,)), ((), ())), preferred_element_type=F32
    ).astype(BF16)


SMEM = pl.BlockSpec(memory_space=pltpu.SMEM)
VMEM = pl.BlockSpec(memory_space=pltpu.VMEM)
HBM = pl.BlockSpec(memory_space=pltpu.HBM)


def in_hbm(value):
    return pltpu.with_memory_space_constraint(value, pltpu.HBM)


def params(limit):
    return pltpu.CompilerParams(vmem_limit_bytes=limit << 20)


def cost(flops, size):
    return pl.CostEstimate(flops=flops, bytes_accessed=size, transcendentals=0)


def in_vmem(value):
    return pltpu.with_memory_space_constraint(value, pltpu.VMEM)


def prefetch(own_t, other_t, own_s, other_s, after):
    (wide_t, columns), wide_s = own_t.shape, own_s.shape[0]
    return pl.pallas_call(
        prefetch_kernel,
        name="prefetch_heads",
        in_specs=[HBM] * (4 + len(after)),
        out_specs=[VMEM] * 2,
        out_shape=[pltpu.VMEM((wide_t, 2 * columns), BF16), pltpu.VMEM((wide_s, 2 * columns), BF16)],
        scratch_shapes=[pltpu.SemaphoreType.DMA((16,))],
        compiler_params=params(2),
        cost_estimate=cost(0, 8 * (wide_t + wide_s) * columns),
    )(*map(in_hbm, (own_t, other_t, own_s, other_s, *after)))


def logits_of(table, place, units, heads_t, heads_s):
    tokens = 8 * HALF
    (wide_t, columns), wide_s = heads_t.shape, heads_s.shape[0]
    logits = pltpu.VMEM((tokens, columns), F32)
    return pl.pallas_call(
        logits_kernel,
        name="logits",
        in_specs=[SMEM, SMEM] + [HBM] * 8 + [VMEM] * 2,
        out_specs=[VMEM, VMEM, HBM, HBM],
        out_shape=[
            logits,
            logits,
            pltpu.HBM((64, 8, tokens), F32),
            pltpu.HBM((tokens, wide_s), BF16),
        ],
        scratch_shapes=[
            pltpu.VMEM((64, *units[0].shape[1:]), BF16),
            pltpu.VMEM((tokens, wide_t), BF16),
            pltpu.VMEM((tokens, wide_s), BF16),
            pltpu.VMEM((tokens, columns), F32),
            pltpu.VMEM((64, 8, tokens), F32),
            pltpu.VMEM((tokens, LANES), F32),
            pltpu.SemaphoreType.DMA((8,)),
            pltpu.SemaphoreType.DMA((2,)),
        ],
        compiler_params=params(24),
        cost_estimate=cost(2 * tokens * (wide_t + wide_s) * columns, 8 << 20),
    )(table, place, *map(in_hbm, units), *map(in_vmem, (heads_t, heads_s)))


def gradient_of(stats, weight, teacher, student, own_s, other_s):
    tokens, columns = teacher.shape
    wide = own_s.shape[0]
    return pl.pallas_call(
        gradient_kernel,
        name="hidden_gradient",
        in_specs=[VMEM] * 4 + [HBM] * 2,
        out_specs=[HBM, HBM, VMEM],
        out_shape=[
            pltpu.HBM((8, 8, HALF, wide // 8), BF16),
            pltpu.HBM((tokens, columns), BF16),
            jax.ShapeDtypeStruct((8, tokens), F32),
        ],
        scratch_shapes=[
            pltpu.VMEM((wide, columns), BF16),
            pltpu.VMEM((8, 8, HALF, wide // 8), BF16),
            pltpu.VMEM((tokens, columns), BF16),
            pltpu.VMEM((tokens, LANES), F32),
            pltpu.SemaphoreType.DMA((8,)),
            pltpu.SemaphoreType.DMA((5,)),
        ],
        compiler_params=params(LIMIT),
        cost_estimate=cost(2 * tokens * wide * columns, 2 * wide * columns),
    )(stats, weight, *map(in_vmem, (teacher, student)), *map(in_hbm, (own_s, other_s)))


def head_gradient_of(own, other, mine, got):
    (tokens, wide), columns = own.shape, got.shape[1]
    width = wide // 8
    strip = pl.BlockSpec((tokens, width), lambda k: (0, k))
    whole = pl.BlockSpec((tokens, columns), lambda k: (0, 0))
    return pl.pallas_call(
        head_kernel,
        name="head_gradient",
        grid=(8,),
        in_specs=[strip, strip, whole, whole],
        out_specs=pl.BlockSpec((width, columns), lambda k: (k, 0)),
        out_shape=jax.ShapeDtypeStruct((wide, columns), BF16),
        compiler_params=params(LIMIT),
        cost_estimate=cost(4 * tokens * wide * columns, 16 << 20),
    )(own, other, mine, got)


def weights(lengths, total_rows):
    seq_count = lengths.shape[0]
    ends = jnp.cumsum(lengths)
    starts = ends - lengths
    position = jnp.arange(total_rows, dtype=jnp.int32)[:, None]
    inside = (position >= starts[None, :]) & (position < ends[None, :])
    seq_len = jnp.sum(jnp.where(inside, lengths[None, :], 0), axis=1)
    return LOSS_SCALE * total_rows / seq_count / seq_len.astype(F32)


def per_device(teacher_hidden, student_hidden, teacher_head, student_head, lengths, sampled):
    group, member = lax.axis_index("grp"), lax.axis_index("vocab")
    core = member % 2
    is_first = core == 0
    wide_t, columns = teacher_head.shape
    wide_s = student_head.shape[0]
    tokens = 8 * HALF
    part_t, part_s = wide_t // 8, wide_s // 8
    strips_t, strips_s = part_t // LANES, part_s // LANES

    got_t, got_s = swap(teacher_hidden), swap(student_hidden)
    teacher_late, student_late, got_t, got_s = lax.optimization_barrier(
        (teacher_head, student_head, got_t, got_s)
    )
    other_teacher_head = swap(teacher_late)
    other_student_head = swap(student_late)

    def half(value):
        value = value.reshape(2, HALF, -1)
        return jnp.where(is_first, value[0], value[1])

    def sides(own, got):
        own, got = half(own), half(got)
        return jnp.where(is_first, own, got), jnp.where(is_first, got, own)

    def strips(a, b, count):
        rows = jnp.concatenate([a, b], axis=1).reshape(HALF, count, LANES)
        return rows.transpose(1, 0, 2).reshape(count * HALF, LANES)

    ids = sampled.reshape(2, HALF)
    ids = jnp.where(is_first, ids[0], ids[1])
    digits = jnp.stack([ids // 4096, (ids // 64) % 64, ids % 64]).astype(BF16)
    digits = jnp.pad(digits, ((0, ID_ROWS - 3), (0, LANES - HALF)))
    block = jnp.concatenate(
        [
            strips(*sides(teacher_hidden, got_t), strips_t),
            digits,
            strips(*sides(student_hidden, got_s), strips_s),
        ]
    )
    near = to_all(block, FIRST)
    units = second_gather(near)
    heads_t, heads_s = prefetch(
        teacher_head, other_teacher_head, student_head, other_student_head, units[1:4]
    )

    tables = jnp.asarray(POSITIONS)
    table = jnp.where(is_first, tables[0], tables[1])
    number_of = group * lax.axis_size("vocab") + member
    place = jnp.stack(
        [number_of * columns, (number_of + 1 - 2 * core) * columns, jnp.asarray(CORNERS)[number_of]]
    ).astype(jnp.int32)
    teacher_logits, student_logits, stats, own_rows = logits_of(table, place, units, heads_t, heads_s)
    other_rows = swap(own_rows)
    all_stats = lax.all_to_all(stats, BOTH, 0, 0, axis_index_groups=SAME_CORE)

    weight = weights(lengths, 2 * tokens).reshape(8, 2, HALF)
    weight = jnp.where(is_first, weight[:, 0], weight[:, 1]).reshape(1, tokens)
    part, grads, kl = gradient_of(
        all_stats, weight, teacher_logits, student_logits, student_head, other_student_head
    )
    got_grad = swap(grads[:, columns:])
    parts = lax.all_to_all(part.reshape(64, HALF, part_s), BOTH, 0, 0, axis_index_groups=SAME_CORE)
    head_grad = head_gradient_of(own_rows, other_rows, grads, got_grad)
    parts, head_grad = lax.optimization_barrier((parts, head_grad))
    hidden = jnp.sum(parts.astype(F32), axis=0).astype(BF16)
    one, two = hidden[:, : part_s // 2], hidden[:, part_s // 2 :]
    kept = jnp.where(is_first, one, two)
    got = swap(jnp.where(is_first, two, one))
    hidden_grad = jnp.concatenate(
        [jnp.where(is_first, kept, got), jnp.where(is_first, got, kept)], axis=0
    )

    def own_tokens(who):
        return lax.dynamic_slice(kl, (0, group * HALF + (4 * who) % HALF), (2, 4))

    got = swap(own_tokens(member + 1 - 2 * core))
    out = jnp.where(member // 8 == core, own_tokens(member), got)
    return head_grad, hidden_grad, out[0], out[1]


def solution(mesh):
    return jax.shard_map(
        per_device,
        mesh=mesh,
        in_specs=(
            P("grp", "vocab"),
            P("grp", "vocab"),
            P(None, BOTH),
            P(None, BOTH),
            P(),
            P("grp"),
        ),
        out_specs=(P(None, BOTH), P("grp", "vocab"), P(BOTH), P(BOTH)),
        check_vma=False,
    )
```

```python
import functools
import itertools

import jax
import jax.numpy as jnp
import numpy as np
from jax import lax
from jax.experimental import pallas as pl
from jax.experimental.pallas import tpu as pltpu
from jax.sharding import PartitionSpec as P

LOSS_SCALE = 16
BOTH = ("grp", "vocab")
F32, BF16 = jnp.float32, jnp.bfloat16
HALF = 32
LANES = 128
ID_ROWS = 16
PIECES = 2
LIMIT = 56
DEPTH = 8
TILE = 256
SHARES = ((0, 1), (2, 3), (4, 5), (6,), (7,))
CORNER_OF = (0, 4, 2, 1, 3, 5, 6, 7)


def device(x, y, z, core):
    return ((x % 2) * 4 + z) * 16 + ((x // 2) * 4 + y) * 2 + core


def cubes(core, step, rank):
    seen, groups = set(), []
    for where in itertools.product(range(4), repeat=3):
        if where in seen:
            continue
        pairs = [sorted((p, p ^ step), key=rank) for p in where]
        members = list(itertools.product(*pairs))
        seen.update(members)
        groups.append([device(*m, core) for m in members])
    return groups


def low(p):
    return p & 1


def high(p):
    return p >> 1


def parity(p):
    return (p & 1) ^ (p >> 1)


FIRST = cubes(0, 1, low) + cubes(1, 3, high)
SAME_CORE = [[2 * chip + core for chip in range(64)] for core in (0, 1)]
SWAP = [(i, i ^ 1) for i in range(128)]


def chips():
    return itertools.product(range(4), repeat=3)


def number(rank, place):
    return rank(place[0]) * 4 + rank(place[1]) * 2 + rank(place[2])


def positions():
    table = np.zeros((2, 64), np.int32)
    for place in chips():
        chip = device(*place, 0) // 2
        table[0, chip] = number(high, place) * 8 + number(low, place)
        table[1, chip] = number(parity, place) * 8 + number(high, place)
    return table


def links(axes):
    pairs = []
    for place in chips():
        for core in (0, 1):
            other = list(place)
            for axis in axes:
                other[axis] ^= (3, 1)[core]
            pairs.append((device(*place, core), device(*other, core)))
    return pairs


POSITIONS = positions()


def swap(value):
    return lax.ppermute(value, BOTH, SWAP)


def to_all(block, groups):
    size = len(groups[0])
    return lax.all_to_all(
        jnp.broadcast_to(block, (size,) + block.shape), BOTH, 0, 0, axis_index_groups=groups
    )


def second_gather(near):
    def along(value, *axes):
        return lax.ppermute(value, BOTH, links(axes))

    one = [along(near, axis) for axis in range(3)]
    far = along(near, 0, 1, 2)
    two = [along(one[(axis + 2) % 3], (axis + 1) % 3) for axis in range(3)]
    return [near, *one, *two, far]


def rows_of(core, blocks_ref, chunk, at, strips):
    parts = [blocks_ref[position(core, group, chunk), at : at + strips * HALF] for group in range(8)]
    return jnp.concatenate(
        [
            jnp.concatenate([p[s * HALF : (s + 1) * HALF] for p in parts], axis=0)
            for s in range(strips)
        ],
        axis=1,
    )


def position(core, group, chunk):
    zero, one = (int(table[group * 8 + chunk]) for table in POSITIONS)
    return zero + core * (one - zero)


class Stream:
    def __init__(self, sems):
        self.sems = sems
        self.copies = []
        self.started = 0

    def add(self, source, target):
        self.copies.append(pltpu.make_async_copy(source, target, self.sems.at[len(self.copies)]))
        return len(self.copies) - 1

    def start(self, count):
        for copy in self.copies[self.started : count]:
            copy.start()
        self.started = max(self.started, min(count, len(self.copies)))

    def wait(self, i):
        self.copies[i].wait()
        self.start(i + 1 + DEPTH)


def put_beside(pairs_and_buffers, sems):
    copies = []
    for pair, buffer in pairs_and_buffers:
        rows, columns = pair[0].shape
        size = rows // 4
        for i in range(4):
            for j, ref in enumerate(pair):
                at = pl.ds(i * size, size)
                copies.append(
                    pltpu.make_async_copy(
                        ref.at[at], buffer.at[at, pl.ds(j * columns, columns)], sems.at[len(copies)]
                    )
                )
                copies[-1].start()
    for copy in copies:
        copy.wait()


def prefetch_kernel(own_t, other_t, own_s, other_s, first, second, third, heads_t, heads_s, sems):
    put_beside([((own_t, other_t), heads_t), ((own_s, other_s), heads_s)], sems)


def logits_kernel(
    place_ref, *refs
):
    units, (heads_t, heads_s, teacher, student, stats_out, lhs_out) = refs[:8], refs[8:14]
    blocks_ref, lhs_t, lhs_s, powers, stats, work, sems, out_sems = refs[14:]
    core = place_ref[3]
    at_s = 4 * HALF + ID_ROWS
    arriving = []
    for part, (at, size) in enumerate(((0, at_s), (at_s, 5 * HALF))):
        for n, unit in enumerate(units):
            start = (place_ref[2] ^ CORNER_OF[n]) * 8
            rows = pl.ds(at, size)
            arriving.append(
                pltpu.make_async_copy(
                    unit.at[:, rows], blocks_ref.at[pl.ds(start, 8), rows], sems.at[part, n]
                )
            )
            arriving[-1].start()
    columns = heads_t.shape[1] // 2
    lane = lax.broadcasted_iota(jnp.int32, (HALF, LANES), 1)
    column = lax.broadcasted_iota(jnp.int32, (HALF, columns), 1)
    column = jnp.concatenate([column + place_ref[0], column + place_ref[1]], axis=1)

    def columns_of(values, first):
        row = jnp.zeros((HALF, LANES), F32)
        for j, value in enumerate(values):
            row = jnp.where(lane == first + j, value, row)
        return row

    def teacher_values(group):
        rows = pl.ds(group * HALF, HALF)
        t = teacher[rows, :]
        top = jnp.max(t, axis=1, keepdims=True)
        t = t - top
        e = jnp.exp(t)
        powers[rows, :] = e
        work[rows, :] = columns_of(
            (top, jnp.sum(e, axis=1, keepdims=True), jnp.sum(e * t, axis=1, keepdims=True)), 0
        )

    for copy in arriving[:8]:
        copy.wait()
    for chunk in range(8):
        lhs_t[:, chunk * 4 * LANES : (chunk + 1) * 4 * LANES] = rows_of(core, blocks_ref, chunk, 0, 4)
    for copy in arriving[8:]:
        copy.wait()
    for j, chunks in enumerate(SHARES):
        at = slice(j * TILE, (j + 1) * TILE)
        teacher[:, at] = jnp.dot(lhs_t[...], heads_t[:, at], preferred_element_type=F32)
        for chunk in chunks:
            lhs_s[:, chunk * 5 * LANES : (chunk + 1) * 5 * LANES] = rows_of(
                core, blocks_ref, chunk, at_s, 5
            )
    leaving = [pltpu.make_async_copy(lhs_s, lhs_out, out_sems.at[0])]
    leaving[0].start()
    for j, groups in enumerate(SHARES):
        at = slice(j * TILE, (j + 1) * TILE)
        student[:, at] = jnp.dot(lhs_s[...], heads_s[:, at], preferred_element_type=F32)
        for group in groups:
            teacher_values(group)
    digits = [blocks_ref[position(core, group, 0), 4 * HALF : at_s].astype(F32) for group in range(8)]
    ids = jnp.concatenate([d[0:1] * 4096.0 + d[1:2] * 64.0 + d[2:3] for d in digits], axis=0)
    ids = jnp.concatenate([ids, jnp.zeros((LANES - 8, LANES), F32)], axis=0).T.astype(jnp.int32)
    for group in range(8):
        rows = pl.ds(group * HALF, HALF)
        s = student[rows, :]
        hit = column == ids[:HALF, group : group + 1]
        picked = jnp.sum(jnp.where(hit, teacher[rows, :] - s, 0.0), axis=1, keepdims=True)
        top = jnp.max(s, axis=1, keepdims=True)
        s = s - top
        log_s = jnp.log(jnp.sum(jnp.exp(s), axis=1, keepdims=True))
        term = jnp.sum(powers[rows, :] * s, axis=1, keepdims=True)
        top_t, sum_t, term_t = (work[rows, j : j + 1] for j in range(3))
        log_t = jnp.log(sum_t)
        ratio = (term_t - term) / sum_t - (log_t - log_s)
        work[rows, :] = columns_of((top_t + log_t, top + log_s, ratio, picked), 0)
    values = work[...].T
    values = [values[j : j + 1, h * LANES : (h + 1) * LANES] for j in range(4) for h in range(2)]
    stats[...] = jnp.broadcast_to(jnp.concatenate(values, axis=0), stats.shape)
    leaving.append(pltpu.make_async_copy(stats, stats_out, out_sems.at[1]))
    leaving[1].start()
    for copy in leaving:
        copy.wait()


def gradient_kernel(
    place_ref, lengths_ref, stats_ref, teacher, student, own_s, other_s, part_out, grads_out, kl_ref,
    heads, part, grads, work, sems, out_sems,
):
    stream = Stream(sems)
    size, columns = own_s.shape[0] // 4, own_s.shape[1]
    for i in range(4):
        at = pl.ds(i * size, size)
        for j, ref in enumerate((own_s, other_s)):
            stream.add(ref.at[at], heads.at[at, pl.ds(j * columns, columns)])
    stream.start(DEPTH)
    part_t, part_s, ratios, picked = (stats_ref[:, 2 * j : 2 * j + 2, :] for j in range(4))

    def log_sum(parts):
        top = jnp.max(parts, axis=0, keepdims=True)
        return top + jnp.log(jnp.sum(jnp.exp(parts - top), axis=0, keepdims=True))

    lse_t, lse_s = log_sum(part_t), log_sum(part_s)
    from_t = part_t - lse_t
    kl = jnp.sum(jnp.exp(from_t) * (ratios + (from_t - (part_s - lse_s))), axis=0)
    lse_t, lse_s = lse_t[0], lse_s[0]
    ratio = jnp.sum(picked, axis=0) - (lse_t - lse_s)

    def row(value):
        return jnp.concatenate([value[0:1], value[1:2]], axis=1)

    tokens = 2 * LANES
    kl_ref[...] = jnp.concatenate([row(kl), row(ratio), jnp.zeros((6, tokens), F32)], axis=0)
    token = lax.broadcasted_iota(jnp.int32, (1, tokens), 1)
    token = token + (token // HALF + place_ref[3]) * HALF
    length, end = jnp.zeros((1, tokens), jnp.int32), jnp.int32(0)
    for i in range(lengths_ref.shape[0]):
        inside = token >= end
        end = end + lengths_ref[i]
        length = jnp.where(inside & (token < end), lengths_ref[i], length)
    weight = (LOSS_SCALE * 2 * tokens / lengths_ref.shape[0]) / length.astype(F32)
    rows = jnp.concatenate([row(lse_t), row(lse_s), weight, jnp.zeros((LANES - 3, tokens), F32)], axis=0)
    work[...] = rows.T

    for i in range(tokens // HALF):
        at = pl.ds(i * HALF, HALF)
        at_t, at_s, weight = (work[at, j : j + 1] for j in range(3))
        grad = weight * (jnp.exp(student[at, :] - at_s) - jnp.exp(teacher[at, :] - at_t))
        grads[at, :] = grad.astype(BF16)
    leaving = [pltpu.make_async_copy(grads, grads_out, out_sems.at[4])]
    leaving[0].start()
    width = part.shape[3]
    chunks = size // width
    for i in range(4):
        stream.wait(2 * i)
        stream.wait(2 * i + 1)
        product = lax.dot_general(
            grads[...], heads[i * size : (i + 1) * size, :], (((1,), (1,)), ((), ())), preferred_element_type=F32
        ).astype(BF16)
        for group in range(8):
            for j in range(chunks):
                part[group, chunks * i + j] = product[
                    group * HALF : (group + 1) * HALF, j * width : (j + 1) * width
                ]
        at = pl.ds(chunks * i, chunks)
        leaving.append(pltpu.make_async_copy(part.at[:, at], part_out.at[:, at], out_sems.at[i]))
        leaving[-1].start()
    for copy in leaving:
        copy.wait()


def head_kernel(own_ref, other_ref, mine_ref, got_ref, out_ref):
    rows = jnp.concatenate([own_ref[...], other_ref[...]], axis=0)
    grad = jnp.concatenate([mine_ref[...], got_ref[...]], axis=0)
    out_ref[...] = lax.dot_general(
        rows, grad, (((0,), (0,)), ((), ())), preferred_element_type=F32
    ).astype(BF16)


SMEM = pl.BlockSpec(memory_space=pltpu.SMEM)
VMEM = pl.BlockSpec(memory_space=pltpu.VMEM)
HBM = pl.BlockSpec(memory_space=pltpu.HBM)


def in_hbm(value):
    return pltpu.with_memory_space_constraint(value, pltpu.HBM)


def params(limit):
    return pltpu.CompilerParams(vmem_limit_bytes=limit << 20)


def cost(flops, size):
    return pl.CostEstimate(flops=flops, bytes_accessed=size, transcendentals=0)


def in_vmem(value):
    return pltpu.with_memory_space_constraint(value, pltpu.VMEM)


def prefetch(own_t, other_t, own_s, other_s, after):
    (wide_t, columns), wide_s = own_t.shape, own_s.shape[0]
    return pl.pallas_call(
        prefetch_kernel,
        name="prefetch_heads",
        in_specs=[HBM] * 4 + [pl.BlockSpec(memory_space=pl.ANY)] * len(after),
        out_specs=[VMEM] * 2,
        out_shape=[pltpu.VMEM((wide_t, 2 * columns), BF16), pltpu.VMEM((wide_s, 2 * columns), BF16)],
        scratch_shapes=[pltpu.SemaphoreType.DMA((16,))],
        compiler_params=params(2),
        cost_estimate=cost(0, 8 * (wide_t + wide_s) * columns),
    )(*map(in_hbm, (own_t, other_t, own_s, other_s)), *after)


def logits_of(place, units, heads_t, heads_s):
    tokens = 8 * HALF
    (wide_t, columns), wide_s = heads_t.shape, heads_s.shape[0]
    logits = pltpu.VMEM((tokens, columns), F32)
    return pl.pallas_call(
        logits_kernel,
        name="logits",
        in_specs=[SMEM] + [HBM] * 8 + [VMEM] * 2,
        out_specs=[VMEM, VMEM, HBM, HBM],
        out_shape=[
            logits,
            logits,
            pltpu.HBM((64, 8, LANES), F32),
            pltpu.HBM((tokens, wide_s), BF16),
        ],
        scratch_shapes=[
            pltpu.VMEM((64, *units[0].shape[1:]), BF16),
            pltpu.VMEM((tokens, wide_t), BF16),
            pltpu.VMEM((tokens, wide_s), BF16),
            pltpu.VMEM((tokens, columns), F32),
            pltpu.VMEM((64, 8, LANES), F32),
            pltpu.VMEM((tokens, LANES), F32),
            pltpu.SemaphoreType.DMA((2, 8)),
            pltpu.SemaphoreType.DMA((2,)),
        ],
        compiler_params=params(24),
        cost_estimate=cost(2 * tokens * (wide_t + wide_s) * columns, 8 << 20),
    )(place, *map(in_hbm, units), *map(in_vmem, (heads_t, heads_s)))


def gradient_of(place, lengths, stats, teacher, student, own_s, other_s):
    tokens, columns = teacher.shape
    wide = own_s.shape[0]
    return pl.pallas_call(
        gradient_kernel,
        name="hidden_gradient",
        in_specs=[SMEM] * 2 + [VMEM] * 3 + [HBM] * 2,
        out_specs=[HBM, HBM, VMEM],
        out_shape=[
            pltpu.HBM((8, 8, HALF, wide // 8), BF16),
            pltpu.HBM((tokens, columns), BF16),
            jax.ShapeDtypeStruct((8, tokens), F32),
        ],
        scratch_shapes=[
            pltpu.VMEM((wide, columns), BF16),
            pltpu.VMEM((8, 8, HALF, wide // 8), BF16),
            pltpu.VMEM((tokens, columns), BF16),
            pltpu.VMEM((tokens, LANES), F32),
            pltpu.SemaphoreType.DMA((8,)),
            pltpu.SemaphoreType.DMA((5,)),
        ],
        compiler_params=params(LIMIT),
        cost_estimate=cost(2 * tokens * wide * columns, 2 * wide * columns),
    )(place, lengths, *map(in_vmem, (stats, teacher, student)), *map(in_hbm, (own_s, other_s)))


def head_gradient_of(own, other, mine, got):
    (tokens, wide), columns = own.shape, got.shape[1]
    width = wide // 8
    strip = pl.BlockSpec((tokens, width), lambda k: (0, k))
    whole = pl.BlockSpec((tokens, columns), lambda k: (0, 0))
    return pl.pallas_call(
        head_kernel,
        name="head_gradient",
        grid=(8,),
        in_specs=[strip, strip, whole, whole],
        out_specs=pl.BlockSpec((width, columns), lambda k: (k, 0)),
        out_shape=jax.ShapeDtypeStruct((wide, columns), BF16),
        compiler_params=params(LIMIT),
        cost_estimate=cost(4 * tokens * wide * columns, 16 << 20),
    )(own, other, mine, got)


def per_device(teacher_hidden, student_hidden, teacher_head, student_head, lengths, sampled):
    group, member = lax.axis_index("grp"), lax.axis_index("vocab")
    core = member % 2
    is_first = core == 0
    wide_t, columns = teacher_head.shape
    wide_s = student_head.shape[0]
    tokens = 8 * HALF
    part_t, part_s = wide_t // 8, wide_s // 8
    strips_t, strips_s = part_t // LANES, part_s // LANES

    got_t, got_s = swap(teacher_hidden), swap(student_hidden)
    teacher_late, student_late, got_t, got_s = lax.optimization_barrier(
        (teacher_head, student_head, got_t, got_s)
    )
    other_teacher_head = swap(teacher_late)
    other_student_head = swap(student_late)

    def half(value):
        value = value.reshape(2, HALF, -1)
        return jnp.where(is_first, value[0], value[1])

    def sides(own, got):
        own, got = half(own), half(got)
        return jnp.where(is_first, own, got), jnp.where(is_first, got, own)

    def strips(a, b, count):
        rows = jnp.concatenate([a, b], axis=1).reshape(HALF, count, LANES)
        return rows.transpose(1, 0, 2).reshape(count * HALF, LANES)

    ids = sampled.reshape(2, HALF)
    ids = jnp.where(is_first, ids[0], ids[1])
    digits = jnp.stack([ids // 4096, (ids // 64) % 64, ids % 64]).astype(BF16)
    digits = jnp.pad(digits, ((0, ID_ROWS - 3), (0, LANES - HALF)))
    block = jnp.concatenate(
        [
            strips(*sides(teacher_hidden, got_t), strips_t),
            digits,
            strips(*sides(student_hidden, got_s), strips_s),
        ]
    )
    near = to_all(block, FIRST)
    units = second_gather(near)
    heads_t, heads_s = prefetch(
        teacher_head, other_teacher_head, student_head, other_student_head, units[1:4]
    )

    number_of = group * lax.axis_size("vocab") + member
    x_high, y, x_low, z = member // 8, member // 2 % 4, group // 4, group % 4
    corner = x_high * 4 + y // 2 * 2 + z // 2
    corner = corner ^ (core * (x_low * 4 + y % 2 * 2 + z % 2))
    place = [number_of * columns, (number_of + 1 - 2 * core) * columns, corner, core]
    place = jnp.stack(place).astype(jnp.int32)
    teacher_logits, student_logits, stats, own_rows = logits_of(place, units, heads_t, heads_s)
    other_rows = swap(own_rows)
    all_stats = lax.all_to_all(stats, BOTH, 0, 0, axis_index_groups=SAME_CORE)

    part, grads, kl = gradient_of(
        place, lengths, all_stats, teacher_logits, student_logits, student_head, other_student_head
    )
    got_grad = swap(grads[:, columns:])
    parts = lax.all_to_all(part.reshape(64, HALF, part_s), BOTH, 0, 0, axis_index_groups=SAME_CORE)
    head_grad = head_gradient_of(own_rows, other_rows, grads, got_grad)
    parts, head_grad = lax.optimization_barrier((parts, head_grad))
    hidden = jnp.sum(parts.astype(F32), axis=0).astype(BF16)
    one, two = hidden[:, : part_s // 2], hidden[:, part_s // 2 :]
    kept = jnp.where(is_first, one, two)
    got = swap(jnp.where(is_first, two, one))
    hidden_grad = jnp.concatenate(
        [jnp.where(is_first, kept, got), jnp.where(is_first, got, kept)], axis=0
    )

    def own_tokens(who):
        return lax.dynamic_slice(kl, (0, group * HALF + (4 * who) % HALF), (2, 4))

    got = swap(own_tokens(member + 1 - 2 * core))
    out = jnp.where(member // 8 == core, own_tokens(member), got)
    return head_grad, hidden_grad, out[0], out[1]


def solution(mesh):
    return jax.shard_map(
        per_device,
        mesh=mesh,
        in_specs=(
            P("grp", "vocab"),
            P("grp", "vocab"),
            P(None, BOTH),
            P(None, BOTH),
            P(),
            P("grp"),
        ),
        out_specs=(P(None, BOTH), P("grp", "vocab"), P(BOTH), P(BOTH)),
        check_vma=False,
    )
```

```python
import functools
import itertools

import jax
import jax.numpy as jnp
import numpy as np
from jax import lax
from jax.experimental import pallas as pl
from jax.experimental.pallas import tpu as pltpu
from jax.sharding import PartitionSpec as P

LOSS_SCALE = 16
BOTH = ("grp", "vocab")
F32, BF16 = jnp.float32, jnp.bfloat16
HALF = 32
LANES = 128
ID_ROWS = 16
PIECES = 2
LIMIT = 56
DEPTH = 8
TILE = 256
SHARES = ((0, 1), (2, 3), (4, 5), (6,), (7,))
CORNER_OF = (0, 4, 2, 1, 3, 5, 6, 7)


def device(x, y, z, core):
    return ((x % 2) * 4 + z) * 16 + ((x // 2) * 4 + y) * 2 + core


def cubes(core, step, rank):
    seen, groups = set(), []
    for where in itertools.product(range(4), repeat=3):
        if where in seen:
            continue
        pairs = [sorted((p, p ^ step), key=rank) for p in where]
        members = list(itertools.product(*pairs))
        seen.update(members)
        groups.append([device(*m, core) for m in members])
    return groups


def low(p):
    return p & 1


def high(p):
    return p >> 1


def parity(p):
    return (p & 1) ^ (p >> 1)


FIRST = cubes(0, 1, low) + cubes(1, 3, high)
SAME_CORE = [[2 * chip + core for chip in range(64)] for core in (0, 1)]
SWAP = [(i, i ^ 1) for i in range(128)]


def chips():
    return itertools.product(range(4), repeat=3)


def number(rank, place):
    return rank(place[0]) * 4 + rank(place[1]) * 2 + rank(place[2])


def positions():
    table = np.zeros((2, 64), np.int32)
    for place in chips():
        chip = device(*place, 0) // 2
        table[0, chip] = number(high, place) * 8 + number(low, place)
        table[1, chip] = number(parity, place) * 8 + number(high, place)
    return table


def links(axes):
    pairs = []
    for place in chips():
        for core in (0, 1):
            other = list(place)
            for axis in axes:
                other[axis] ^= (3, 1)[core]
            pairs.append((device(*place, core), device(*other, core)))
    return pairs


POSITIONS = positions()


def swap(value):
    return lax.ppermute(value, BOTH, SWAP)


def to_all(block, groups):
    size = len(groups[0])
    return lax.all_to_all(
        jnp.broadcast_to(block, (size,) + block.shape), BOTH, 0, 0, axis_index_groups=groups
    )


def second_gather(near):
    def along(value, *axes):
        return lax.ppermute(value, BOTH, links(axes))

    one = [along(near, axis) for axis in range(3)]
    far = along(near, 0, 1, 2)
    two = [along(one[(axis + 2) % 3], (axis + 1) % 3) for axis in range(3)]
    return [near, *one, *two, far]


def rows_of(core, blocks_ref, chunk, at, strips):
    parts = [blocks_ref[position(core, group, chunk), at : at + strips * HALF] for group in range(8)]
    return jnp.concatenate(
        [
            jnp.concatenate([p[s * HALF : (s + 1) * HALF] for p in parts], axis=0)
            for s in range(strips)
        ],
        axis=1,
    )


def position(core, group, chunk):
    zero, one = (int(table[group * 8 + chunk]) for table in POSITIONS)
    return zero + core * (one - zero)


class Stream:
    def __init__(self, sems):
        self.sems = sems
        self.copies = []
        self.started = 0

    def add(self, source, target):
        self.copies.append(pltpu.make_async_copy(source, target, self.sems.at[len(self.copies)]))
        return len(self.copies) - 1

    def start(self, count):
        for copy in self.copies[self.started : count]:
            copy.start()
        self.started = max(self.started, min(count, len(self.copies)))

    def wait(self, i):
        self.copies[i].wait()
        self.start(i + 1 + DEPTH)


def put_beside(pairs_and_buffers, sems):
    copies = []
    for pair, buffer in pairs_and_buffers:
        rows, columns = pair[0].shape
        size = rows // 4
        for i in range(4):
            for j, ref in enumerate(pair):
                at = pl.ds(i * size, size)
                copies.append(
                    pltpu.make_async_copy(
                        ref.at[at], buffer.at[at, pl.ds(j * columns, columns)], sems.at[len(copies)]
                    )
                )
                copies[-1].start()
    for copy in copies:
        copy.wait()


def prefetch_kernel(own_t, other_t, own_s, other_s, first, second, third, heads_t, heads_s, sems):
    put_beside([((own_t, other_t), heads_t), ((own_s, other_s), heads_s)], sems)


def logits_kernel(
    place_ref, *refs
):
    units, (heads_t, heads_s, teacher, student, stats_out, lhs_out) = refs[:8], refs[8:14]
    blocks_ref, lhs_t, lhs_s, powers, stats, work, sems, out_sems = refs[14:]
    core = place_ref[3]
    at_s = 4 * HALF + ID_ROWS
    arriving = []
    for part, (at, size) in enumerate(((0, at_s), (at_s, 5 * HALF))):
        for n, unit in enumerate(units):
            start = (place_ref[2] ^ CORNER_OF[n]) * 8
            rows = pl.ds(at, size)
            arriving.append(
                pltpu.make_async_copy(
                    unit.at[:, rows], blocks_ref.at[pl.ds(start, 8), rows], sems.at[part, n]
                )
            )
            arriving[-1].start()
    columns = heads_t.shape[1] // 2
    lane = lax.broadcasted_iota(jnp.int32, (HALF, LANES), 1)
    column = lax.broadcasted_iota(jnp.int32, (HALF, columns), 1)
    column = jnp.concatenate([column + place_ref[0], column + place_ref[1]], axis=1)

    def columns_of(values, first):
        row = jnp.zeros((HALF, LANES), F32)
        for j, value in enumerate(values):
            row = jnp.where(lane == first + j, value, row)
        return row

    def teacher_values(group):
        rows = pl.ds(group * HALF, HALF)
        t = teacher[rows, :]
        top = jnp.max(t, axis=1, keepdims=True)
        t = t - top
        e = jnp.exp(t)
        powers[rows, :] = e
        work[rows, :] = columns_of(
            (top, jnp.sum(e, axis=1, keepdims=True), jnp.sum(e * t, axis=1, keepdims=True)), 0
        )

    for copy in arriving[:8]:
        copy.wait()
    for chunk in range(8):
        lhs_t[:, chunk * 4 * LANES : (chunk + 1) * 4 * LANES] = rows_of(core, blocks_ref, chunk, 0, 4)
    for copy in arriving[8:]:
        copy.wait()
    for j, chunks in enumerate(SHARES):
        at = slice(j * TILE, (j + 1) * TILE)
        teacher[:, at] = jnp.dot(lhs_t[...], heads_t[:, at], preferred_element_type=F32)
        for chunk in chunks:
            lhs_s[:, chunk * 5 * LANES : (chunk + 1) * 5 * LANES] = rows_of(
                core, blocks_ref, chunk, at_s, 5
            )
    leaving = [pltpu.make_async_copy(lhs_s, lhs_out, out_sems.at[0])]
    leaving[0].start()
    for j, groups in enumerate(SHARES):
        at = slice(j * TILE, (j + 1) * TILE)
        student[:, at] = jnp.dot(lhs_s[...], heads_s[:, at], preferred_element_type=F32)
        for group in groups:
            teacher_values(group)
    digits = [blocks_ref[position(core, group, 0), 4 * HALF : at_s].astype(F32) for group in range(8)]
    ids = jnp.concatenate([d[0:1] * 4096.0 + d[1:2] * 64.0 + d[2:3] for d in digits], axis=0)
    ids = jnp.concatenate([ids, jnp.zeros((LANES - 8, LANES), F32)], axis=0).T.astype(jnp.int32)
    for group in range(8):
        rows = pl.ds(group * HALF, HALF)
        s = student[rows, :]
        hit = column == ids[:HALF, group : group + 1]
        picked = jnp.sum(jnp.where(hit, teacher[rows, :] - s, 0.0), axis=1, keepdims=True)
        top = jnp.max(s, axis=1, keepdims=True)
        s = s - top
        log_s = jnp.log(jnp.sum(jnp.exp(s), axis=1, keepdims=True))
        term = jnp.sum(powers[rows, :] * s, axis=1, keepdims=True)
        top_t, sum_t, term_t = (work[rows, j : j + 1] for j in range(3))
        log_t = jnp.log(sum_t)
        ratio = (term_t - term) / sum_t - (log_t - log_s)
        work[rows, :] = columns_of((top_t + log_t, top + log_s, ratio, picked), 0)
    values = work[...].T
    values = [values[j : j + 1, h * LANES : (h + 1) * LANES] for j in range(4) for h in range(2)]
    stats[...] = jnp.broadcast_to(jnp.concatenate(values, axis=0), stats.shape)
    leaving.append(pltpu.make_async_copy(stats, stats_out, out_sems.at[1]))
    leaving[1].start()
    for copy in leaving:
        copy.wait()


def gradient_kernel(
    place_ref, lengths_ref, stats_ref, teacher, student, own_s, other_s, part_out, grads_out, kl_ref,
    heads, part, grads, work, sems, out_sems,
):
    stream = Stream(sems)
    size, columns = own_s.shape[0] // 4, own_s.shape[1]
    for i in range(4):
        at = pl.ds(i * size, size)
        for j, ref in enumerate((own_s, other_s)):
            stream.add(ref.at[at], heads.at[at, pl.ds(j * columns, columns)])
    stream.start(DEPTH)
    part_t, part_s, ratios, picked = (stats_ref[:, 2 * j : 2 * j + 2, :] for j in range(4))

    def log_sum(parts):
        top = jnp.max(parts, axis=0, keepdims=True)
        return top + jnp.log(jnp.sum(jnp.exp(parts - top), axis=0, keepdims=True))

    lse_t, lse_s = log_sum(part_t), log_sum(part_s)
    from_t = part_t - lse_t
    kl = jnp.sum(jnp.exp(from_t) * (ratios + (from_t - (part_s - lse_s))), axis=0)
    lse_t, lse_s = lse_t[0], lse_s[0]
    ratio = jnp.sum(picked, axis=0) - (lse_t - lse_s)

    def row(value):
        return jnp.concatenate([value[0:1], value[1:2]], axis=1)

    tokens = 2 * LANES
    kl_ref[...] = jnp.concatenate([row(kl), row(ratio), jnp.zeros((6, tokens), F32)], axis=0)
    token = lax.broadcasted_iota(jnp.int32, (1, tokens), 1)
    token = token + (token // HALF + place_ref[3]) * HALF
    length, end = jnp.zeros((1, tokens), jnp.int32), jnp.int32(0)
    for i in range(lengths_ref.shape[0]):
        inside = token >= end
        end = end + lengths_ref[i]
        length = jnp.where(inside & (token < end), lengths_ref[i], length)
    weight = (LOSS_SCALE * 2 * tokens / lengths_ref.shape[0]) / length.astype(F32)
    rows = jnp.concatenate([row(lse_t), row(lse_s), weight, jnp.zeros((LANES - 3, tokens), F32)], axis=0)
    work[...] = rows.T

    for i in range(tokens // HALF):
        at = pl.ds(i * HALF, HALF)
        at_t, at_s, weight = (work[at, j : j + 1] for j in range(3))
        grad = weight * (jnp.exp(student[at, :] - at_s) - jnp.exp(teacher[at, :] - at_t))
        grads[at, :] = grad.astype(BF16)
    leaving = [pltpu.make_async_copy(grads, grads_out, out_sems.at[4])]
    leaving[0].start()
    width = part.shape[3]
    chunks = size // width
    for i in range(4):
        stream.wait(2 * i)
        stream.wait(2 * i + 1)
        product = lax.dot_general(
            grads[...], heads[i * size : (i + 1) * size, :], (((1,), (1,)), ((), ())), preferred_element_type=F32
        ).astype(BF16)
        for group in range(8):
            for j in range(chunks):
                part[group, chunks * i + j] = product[
                    group * HALF : (group + 1) * HALF, j * width : (j + 1) * width
                ]
        at = pl.ds(chunks * i, chunks)
        leaving.append(pltpu.make_async_copy(part.at[:, at], part_out.at[:, at], out_sems.at[i]))
        leaving[-1].start()
    for copy in leaving:
        copy.wait()


def head_kernel(own_ref, other_ref, mine_ref, got_ref, out_ref):
    rows = jnp.concatenate([own_ref[...], other_ref[...]], axis=0)
    grad = jnp.concatenate([mine_ref[...], got_ref[...]], axis=0)
    out_ref[...] = lax.dot_general(
        rows, grad, (((0,), (0,)), ((), ())), preferred_element_type=F32
    ).astype(BF16)


SMEM = pl.BlockSpec(memory_space=pltpu.SMEM)
VMEM = pl.BlockSpec(memory_space=pltpu.VMEM)
HBM = pl.BlockSpec(memory_space=pltpu.HBM)


def in_hbm(value):
    return pltpu.with_memory_space_constraint(value, pltpu.HBM)


def params(limit):
    return pltpu.CompilerParams(vmem_limit_bytes=limit << 20)


def cost(flops, size):
    return pl.CostEstimate(flops=flops, bytes_accessed=size, transcendentals=0)


def in_vmem(value):
    return pltpu.with_memory_space_constraint(value, pltpu.VMEM)


def prefetch(own_t, other_t, own_s, other_s, after):
    (wide_t, columns), wide_s = own_t.shape, own_s.shape[0]
    return pl.pallas_call(
        prefetch_kernel,
        name="prefetch_heads",
        in_specs=[HBM] * 4 + [pl.BlockSpec(memory_space=pl.ANY)] * len(after),
        out_specs=[VMEM] * 2,
        out_shape=[pltpu.VMEM((wide_t, 2 * columns), BF16), pltpu.VMEM((wide_s, 2 * columns), BF16)],
        scratch_shapes=[pltpu.SemaphoreType.DMA((16,))],
        compiler_params=params(2),
        cost_estimate=cost(0, 8 * (wide_t + wide_s) * columns),
    )(*map(in_hbm, (own_t, other_t, own_s, other_s)), *after)


def logits_of(place, units, heads_t, heads_s):
    tokens = 8 * HALF
    (wide_t, columns), wide_s = heads_t.shape, heads_s.shape[0]
    logits = pltpu.VMEM((tokens, columns), F32)
    return pl.pallas_call(
        logits_kernel,
        name="logits",
        in_specs=[SMEM] + [HBM] * 8 + [VMEM] * 2,
        out_specs=[VMEM, VMEM, HBM, HBM],
        out_shape=[
            logits,
            logits,
            pltpu.HBM((64, 8, LANES), F32),
            pltpu.HBM((tokens, wide_s), BF16),
        ],
        scratch_shapes=[
            pltpu.VMEM((64, *units[0].shape[1:]), BF16),
            pltpu.VMEM((tokens, wide_t), BF16),
            pltpu.VMEM((tokens, wide_s), BF16),
            pltpu.VMEM((tokens, columns), F32),
            pltpu.VMEM((64, 8, LANES), F32),
            pltpu.VMEM((tokens, LANES), F32),
            pltpu.SemaphoreType.DMA((2, 8)),
            pltpu.SemaphoreType.DMA((2,)),
        ],
        compiler_params=params(24),
        cost_estimate=cost(2 * tokens * (wide_t + wide_s) * columns, 8 << 20),
    )(place, *map(in_hbm, units), *map(in_vmem, (heads_t, heads_s)))


def gradient_of(place, lengths, stats, teacher, student, own_s, other_s):
    tokens, columns = teacher.shape
    wide = own_s.shape[0]
    return pl.pallas_call(
        gradient_kernel,
        name="hidden_gradient",
        in_specs=[SMEM] * 2 + [VMEM] * 3 + [HBM] * 2,
        out_specs=[HBM, HBM, VMEM],
        out_shape=[
            pltpu.HBM((8, 8, HALF, wide // 8), BF16),
            pltpu.HBM((tokens, columns), BF16),
            jax.ShapeDtypeStruct((8, tokens), F32),
        ],
        scratch_shapes=[
            pltpu.VMEM((wide, columns), BF16),
            pltpu.VMEM((8, 8, HALF, wide // 8), BF16),
            pltpu.VMEM((tokens, columns), BF16),
            pltpu.VMEM((tokens, LANES), F32),
            pltpu.SemaphoreType.DMA((8,)),
            pltpu.SemaphoreType.DMA((5,)),
        ],
        compiler_params=params(LIMIT),
        cost_estimate=cost(2 * tokens * wide * columns, 2 * wide * columns),
    )(place, lengths, *map(in_vmem, (stats, teacher, student)), *map(in_hbm, (own_s, other_s)))


def head_gradient_of(own, other, mine, got):
    (tokens, wide), columns = own.shape, got.shape[1]
    width = wide // 8
    strip = pl.BlockSpec((tokens, width), lambda k: (0, k))
    whole = pl.BlockSpec((tokens, columns), lambda k: (0, 0))
    return pl.pallas_call(
        head_kernel,
        name="head_gradient",
        grid=(8,),
        in_specs=[strip, strip, whole, whole],
        out_specs=pl.BlockSpec((width, columns), lambda k: (k, 0)),
        out_shape=jax.ShapeDtypeStruct((wide, columns), BF16),
        compiler_params=params(LIMIT),
        cost_estimate=cost(4 * tokens * wide * columns, 16 << 20),
    )(own, other, mine, got)


def per_device(teacher_hidden, student_hidden, teacher_head, student_head, lengths, sampled):
    group, member = lax.axis_index("grp"), lax.axis_index("vocab")
    core = member % 2
    is_first = core == 0
    wide_t, columns = teacher_head.shape
    wide_s = student_head.shape[0]
    tokens = 8 * HALF
    part_t, part_s = wide_t // 8, wide_s // 8
    strips_t, strips_s = part_t // LANES, part_s // LANES

    got_t, got_s = swap(teacher_hidden), swap(student_hidden)
    teacher_late, got_t, got_s = lax.optimization_barrier((teacher_head, got_t, got_s))
    other_teacher_head = swap(teacher_late)

    def half(value):
        value = value.reshape(2, HALF, -1)
        return jnp.where(is_first, value[0], value[1])

    def sides(own, got):
        own, got = half(own), half(got)
        return jnp.where(is_first, own, got), jnp.where(is_first, got, own)

    def strips(a, b, count):
        rows = jnp.concatenate([a, b], axis=1).reshape(HALF, count, LANES)
        return rows.transpose(1, 0, 2).reshape(count * HALF, LANES)

    ids = sampled.reshape(2, HALF)
    ids = jnp.where(is_first, ids[0], ids[1])
    digits = jnp.stack([ids // 4096, (ids // 64) % 64, ids % 64]).astype(BF16)
    digits = jnp.pad(digits, ((0, ID_ROWS - 3), (0, LANES - HALF)))
    block = jnp.concatenate(
        [
            strips(*sides(teacher_hidden, got_t), strips_t),
            digits,
            strips(*sides(student_hidden, got_s), strips_s),
        ]
    )
    near = to_all(block, FIRST)
    near, other_teacher_head, student_late = lax.optimization_barrier((near, other_teacher_head, student_head))
    other_student_head = swap(student_late)
    units = second_gather(near)
    heads_t, heads_s = prefetch(
        teacher_head, other_teacher_head, student_head, other_student_head, units[1:4]
    )

    number_of = group * lax.axis_size("vocab") + member
    x_high, y, x_low, z = member // 8, member // 2 % 4, group // 4, group % 4
    corner = x_high * 4 + y // 2 * 2 + z // 2
    corner = corner ^ (core * (x_low * 4 + y % 2 * 2 + z % 2))
    place = [number_of * columns, (number_of + 1 - 2 * core) * columns, corner, core]
    place = jnp.stack(place).astype(jnp.int32)
    teacher_logits, student_logits, stats, own_rows = logits_of(place, units, heads_t, heads_s)
    other_rows = swap(own_rows)
    all_stats = lax.all_to_all(stats, BOTH, 0, 0, axis_index_groups=SAME_CORE)

    part, grads, kl = gradient_of(
        place, lengths, all_stats, teacher_logits, student_logits, student_head, other_student_head
    )
    got_grad = swap(grads[:, columns:])
    parts = lax.all_to_all(part.reshape(64, HALF, part_s), BOTH, 0, 0, axis_index_groups=SAME_CORE)
    head_grad = head_gradient_of(own_rows, other_rows, grads, got_grad)
    parts, head_grad = lax.optimization_barrier((parts, head_grad))
    hidden = jnp.sum(parts.astype(F32), axis=0).astype(BF16)
    one, two = hidden[:, : part_s // 2], hidden[:, part_s // 2 :]
    kept = jnp.where(is_first, one, two)
    got = swap(jnp.where(is_first, two, one))
    hidden_grad = jnp.concatenate(
        [jnp.where(is_first, kept, got), jnp.where(is_first, got, kept)], axis=0
    )

    def own_tokens(who):
        return lax.dynamic_slice(kl, (0, group * HALF + (4 * who) % HALF), (2, 4))

    got = swap(own_tokens(member + 1 - 2 * core))
    out = jnp.where(member // 8 == core, own_tokens(member), got)
    return head_grad, hidden_grad, out[0], out[1]


def solution(mesh):
    return jax.shard_map(
        per_device,
        mesh=mesh,
        in_specs=(
            P("grp", "vocab"),
            P("grp", "vocab"),
            P(None, BOTH),
            P(None, BOTH),
            P(),
            P("grp"),
        ),
        out_specs=(P(None, BOTH), P("grp", "vocab"), P(BOTH), P(BOTH)),
        check_vma=False,
    )
```

```python
import functools
import itertools

import jax
import jax.numpy as jnp
import numpy as np
from jax import lax
from jax.experimental import pallas as pl
from jax.experimental.pallas import tpu as pltpu
from jax.sharding import PartitionSpec as P

LOSS_SCALE = 16
BOTH = ("grp", "vocab")
F32, BF16 = jnp.float32, jnp.bfloat16
HALF = 32
LANES = 128
ID_ROWS = 16
PIECES = 2
LIMIT = 56
DEPTH = 8
TILE = 256
SHARES = ((), (0, 1), (2, 3), (4, 5), (6, 7))
CORNER_OF = (0, 4, 2, 1, 3, 5, 6, 7)


def device(x, y, z, core):
    return ((x % 2) * 4 + z) * 16 + ((x // 2) * 4 + y) * 2 + core


def cubes(core, step, rank):
    seen, groups = set(), []
    for where in itertools.product(range(4), repeat=3):
        if where in seen:
            continue
        pairs = [sorted((p, p ^ step), key=rank) for p in where]
        members = list(itertools.product(*pairs))
        seen.update(members)
        groups.append([device(*m, core) for m in members])
    return groups


def low(p):
    return p & 1


def high(p):
    return p >> 1


def parity(p):
    return (p & 1) ^ (p >> 1)


FIRST = cubes(0, 1, low) + cubes(1, 3, high)
SAME_CORE = [[2 * chip + core for chip in range(64)] for core in (0, 1)]
SWAP = [(i, i ^ 1) for i in range(128)]


def chips():
    return itertools.product(range(4), repeat=3)


def number(rank, place):
    return rank(place[0]) * 4 + rank(place[1]) * 2 + rank(place[2])


def positions():
    table = np.zeros((2, 64), np.int32)
    for place in chips():
        chip = device(*place, 0) // 2
        table[0, chip] = number(high, place) * 8 + number(low, place)
        table[1, chip] = number(parity, place) * 8 + number(high, place)
    return table


def links(axes):
    pairs = []
    for place in chips():
        for core in (0, 1):
            other = list(place)
            for axis in axes:
                other[axis] ^= (3, 1)[core]
            pairs.append((device(*place, core), device(*other, core)))
    return pairs


POSITIONS = positions()


def swap(value):
    return lax.ppermute(value, BOTH, SWAP)


def to_all(block, groups):
    size = len(groups[0])
    return lax.all_to_all(
        jnp.broadcast_to(block, (size,) + block.shape), BOTH, 0, 0, axis_index_groups=groups
    )


def second_gather(near):
    def along(value, *axes):
        return lax.ppermute(value, BOTH, links(axes))

    one = [along(near, axis) for axis in range(3)]
    far = along(near, 0, 1, 2)
    two = [along(one[(axis + 2) % 3], (axis + 1) % 3) for axis in range(3)]
    return [near, *one, *two, far]


def rows_of(core, blocks_ref, chunk, at, strips):
    parts = [blocks_ref[position(core, group, chunk), at : at + strips * HALF] for group in range(8)]
    return jnp.concatenate(
        [
            jnp.concatenate([p[s * HALF : (s + 1) * HALF] for p in parts], axis=0)
            for s in range(strips)
        ],
        axis=1,
    )


def position(core, group, chunk):
    zero, one = (int(table[group * 8 + chunk]) for table in POSITIONS)
    return zero + core * (one - zero)


class Stream:
    def __init__(self, sems):
        self.sems = sems
        self.copies = []
        self.started = 0

    def add(self, source, target):
        self.copies.append(pltpu.make_async_copy(source, target, self.sems.at[len(self.copies)]))
        return len(self.copies) - 1

    def start(self, count):
        for copy in self.copies[self.started : count]:
            copy.start()
        self.started = max(self.started, min(count, len(self.copies)))

    def wait(self, i):
        self.copies[i].wait()
        self.start(i + 1 + DEPTH)


def put_beside(pairs_and_buffers, sems):
    copies = []
    for pair, buffer in pairs_and_buffers:
        rows, columns = pair[0].shape
        size = rows // 4
        for i in range(4):
            for j, ref in enumerate(pair):
                at = pl.ds(i * size, size)
                copies.append(
                    pltpu.make_async_copy(
                        ref.at[at], buffer.at[at, pl.ds(j * columns, columns)], sems.at[len(copies)]
                    )
                )
                copies[-1].start()
    for copy in copies:
        copy.wait()


def prefetch_kernel(own_t, other_t, own_s, other_s, first, second, third, heads_t, heads_s, sems):
    put_beside([((own_t, other_t), heads_t), ((own_s, other_s), heads_s)], sems)


def logits_kernel(
    place_ref, *refs
):
    units, (heads_t, heads_s, teacher, student, stats_out, lhs_out) = refs[:8], refs[8:14]
    blocks_ref, lhs_t, lhs_s, powers, stats, work, sems, out_sems = refs[14:]
    core = place_ref[3]
    at_s = 4 * HALF + ID_ROWS
    arriving = []
    for part, (at, size) in enumerate(((0, at_s), (at_s, 5 * HALF))):
        for n, unit in enumerate(units):
            start = (place_ref[2] ^ CORNER_OF[n]) * 8
            rows = pl.ds(at, size)
            arriving.append(
                pltpu.make_async_copy(
                    unit.at[:, rows], blocks_ref.at[pl.ds(start, 8), rows], sems.at[part, n]
                )
            )
    for copy in arriving[:8]:
        copy.start()
    columns = heads_t.shape[1] // 2
    lane = lax.broadcasted_iota(jnp.int32, (HALF, LANES), 1)
    column = lax.broadcasted_iota(jnp.int32, (HALF, columns), 1)
    column = jnp.concatenate([column + place_ref[0], column + place_ref[1]], axis=1)

    def columns_of(values, first):
        row = jnp.zeros((HALF, LANES), F32)
        for j, value in enumerate(values):
            row = jnp.where(lane == first + j, value, row)
        return row

    def teacher_values(group):
        rows = pl.ds(group * HALF, HALF)
        t = teacher[rows, :]
        top = jnp.max(t, axis=1, keepdims=True)
        t = t - top
        e = jnp.exp(t)
        powers[rows, :] = e
        work[rows, :] = columns_of(
            (top, jnp.sum(e, axis=1, keepdims=True), jnp.sum(e * t, axis=1, keepdims=True)), 0
        )

    for copy in arriving[:8]:
        copy.wait()
    for copy in arriving[8:]:
        copy.start()
    for chunk in range(8):
        lhs_t[:, chunk * 4 * LANES : (chunk + 1) * 4 * LANES] = rows_of(core, blocks_ref, chunk, 0, 4)
    for j, chunks in enumerate(SHARES):
        at = slice(j * TILE, (j + 1) * TILE)
        teacher[:, at] = jnp.dot(lhs_t[...], heads_t[:, at], preferred_element_type=F32)
        if j == 1:
            for copy in arriving[8:]:
                copy.wait()
        for chunk in chunks:
            lhs_s[:, chunk * 5 * LANES : (chunk + 1) * 5 * LANES] = rows_of(
                core, blocks_ref, chunk, at_s, 5
            )
    leaving = [pltpu.make_async_copy(lhs_s, lhs_out, out_sems.at[0])]
    leaving[0].start()
    for j, groups in enumerate(SHARES):
        at = slice(j * TILE, (j + 1) * TILE)
        student[:, at] = jnp.dot(lhs_s[...], heads_s[:, at], preferred_element_type=F32)
        for group in groups:
            teacher_values(group)
    digits = [blocks_ref[position(core, group, 0), 4 * HALF : at_s].astype(F32) for group in range(8)]
    ids = jnp.concatenate([d[0:1] * 4096.0 + d[1:2] * 64.0 + d[2:3] for d in digits], axis=0)
    ids = jnp.concatenate([ids, jnp.zeros((LANES - 8, LANES), F32)], axis=0).T.astype(jnp.int32)
    for group in range(8):
        rows = pl.ds(group * HALF, HALF)
        s = student[rows, :]
        hit = column == ids[:HALF, group : group + 1]
        picked = jnp.sum(jnp.where(hit, teacher[rows, :] - s, 0.0), axis=1, keepdims=True)
        top = jnp.max(s, axis=1, keepdims=True)
        s = s - top
        log_s = jnp.log(jnp.sum(jnp.exp(s), axis=1, keepdims=True))
        term = jnp.sum(powers[rows, :] * s, axis=1, keepdims=True)
        top_t, sum_t, term_t = (work[rows, j : j + 1] for j in range(3))
        log_t = jnp.log(sum_t)
        ratio = (term_t - term) / sum_t - (log_t - log_s)
        work[rows, :] = columns_of((top_t + log_t, top + log_s, ratio, picked), 0)
    values = work[...].T
    values = [values[j : j + 1, h * LANES : (h + 1) * LANES] for j in range(4) for h in range(2)]
    stats[...] = jnp.broadcast_to(jnp.concatenate(values, axis=0), stats.shape)
    leaving.append(pltpu.make_async_copy(stats, stats_out, out_sems.at[1]))
    leaving[1].start()
    for copy in leaving:
        copy.wait()


def gradient_kernel(
    place_ref, lengths_ref, stats_ref, teacher, student, own_s, other_s, part_out, grads_out, kl_ref,
    heads, part, grads, work, sems, out_sems,
):
    stream = Stream(sems)
    size, columns = own_s.shape[0] // 4, own_s.shape[1]
    for i in range(4):
        at = pl.ds(i * size, size)
        for j, ref in enumerate((own_s, other_s)):
            stream.add(ref.at[at], heads.at[at, pl.ds(j * columns, columns)])
    stream.start(DEPTH)
    part_t, part_s, ratios, picked = (stats_ref[:, 2 * j : 2 * j + 2, :] for j in range(4))

    def log_sum(parts):
        top = jnp.max(parts, axis=0, keepdims=True)
        return top + jnp.log(jnp.sum(jnp.exp(parts - top), axis=0, keepdims=True))

    lse_t, lse_s = log_sum(part_t), log_sum(part_s)
    from_t = part_t - lse_t
    kl = jnp.sum(jnp.exp(from_t) * (ratios + (from_t - (part_s - lse_s))), axis=0)
    lse_t, lse_s = lse_t[0], lse_s[0]
    ratio = jnp.sum(picked, axis=0) - (lse_t - lse_s)

    def row(value):
        return jnp.concatenate([value[0:1], value[1:2]], axis=1)

    tokens = 2 * LANES
    kl_ref[...] = jnp.concatenate([row(kl), row(ratio), jnp.zeros((6, tokens), F32)], axis=0)
    token = lax.broadcasted_iota(jnp.int32, (1, tokens), 1)
    token = token + (token // HALF + place_ref[3]) * HALF
    length, end = jnp.zeros((1, tokens), jnp.int32), jnp.int32(0)
    for i in range(lengths_ref.shape[0]):
        inside = token >= end
        end = end + lengths_ref[i]
        length = jnp.where(inside & (token < end), lengths_ref[i], length)
    weight = (LOSS_SCALE * 2 * tokens / lengths_ref.shape[0]) / length.astype(F32)
    rows = jnp.concatenate([row(lse_t), row(lse_s), weight, jnp.zeros((LANES - 3, tokens), F32)], axis=0)
    work[...] = rows.T

    for i in range(tokens // HALF):
        at = pl.ds(i * HALF, HALF)
        at_t, at_s, weight = (work[at, j : j + 1] for j in range(3))
        grad = weight * (jnp.exp(student[at, :] - at_s) - jnp.exp(teacher[at, :] - at_t))
        grads[at, :] = grad.astype(BF16)
    leaving = [pltpu.make_async_copy(grads, grads_out, out_sems.at[4])]
    leaving[0].start()
    width = part.shape[3]
    chunks = size // width
    for i in range(4):
        stream.wait(2 * i)
        stream.wait(2 * i + 1)
        product = lax.dot_general(
            grads[...], heads[i * size : (i + 1) * size, :], (((1,), (1,)), ((), ())), preferred_element_type=F32
        ).astype(BF16)
        for group in range(8):
            for j in range(chunks):
                part[group, chunks * i + j] = product[
                    group * HALF : (group + 1) * HALF, j * width : (j + 1) * width
                ]
        at = pl.ds(chunks * i, chunks)
        leaving.append(pltpu.make_async_copy(part.at[:, at], part_out.at[:, at], out_sems.at[i]))
        leaving[-1].start()
    for copy in leaving:
        copy.wait()


def head_kernel(own_ref, other_ref, mine_ref, got_ref, out_ref):
    rows = jnp.concatenate([own_ref[...], other_ref[...]], axis=0)
    grad = jnp.concatenate([mine_ref[...], got_ref[...]], axis=0)
    out_ref[...] = lax.dot_general(
        rows, grad, (((0,), (0,)), ((), ())), preferred_element_type=F32
    ).astype(BF16)


SMEM = pl.BlockSpec(memory_space=pltpu.SMEM)
VMEM = pl.BlockSpec(memory_space=pltpu.VMEM)
HBM = pl.BlockSpec(memory_space=pltpu.HBM)


def in_hbm(value):
    return pltpu.with_memory_space_constraint(value, pltpu.HBM)


def params(limit):
    return pltpu.CompilerParams(vmem_limit_bytes=limit << 20)


def cost(flops, size):
    return pl.CostEstimate(flops=flops, bytes_accessed=size, transcendentals=0)


def in_vmem(value):
    return pltpu.with_memory_space_constraint(value, pltpu.VMEM)


def prefetch(own_t, other_t, own_s, other_s, after):
    (wide_t, columns), wide_s = own_t.shape, own_s.shape[0]
    return pl.pallas_call(
        prefetch_kernel,
        name="prefetch_heads",
        in_specs=[HBM] * 4 + [pl.BlockSpec(memory_space=pl.ANY)] * len(after),
        out_specs=[VMEM] * 2,
        out_shape=[pltpu.VMEM((wide_t, 2 * columns), BF16), pltpu.VMEM((wide_s, 2 * columns), BF16)],
        scratch_shapes=[pltpu.SemaphoreType.DMA((16,))],
        compiler_params=params(2),
        cost_estimate=cost(0, 8 * (wide_t + wide_s) * columns),
    )(*map(in_hbm, (own_t, other_t, own_s, other_s)), *after)


def logits_of(place, units, heads_t, heads_s):
    tokens = 8 * HALF
    (wide_t, columns), wide_s = heads_t.shape, heads_s.shape[0]
    logits = pltpu.VMEM((tokens, columns), F32)
    return pl.pallas_call(
        logits_kernel,
        name="logits",
        in_specs=[SMEM] + [HBM] * 8 + [VMEM] * 2,
        out_specs=[VMEM, VMEM, HBM, HBM],
        out_shape=[
            logits,
            logits,
            pltpu.HBM((64, 8, LANES), F32),
            pltpu.HBM((tokens, wide_s), BF16),
        ],
        scratch_shapes=[
            pltpu.VMEM((64, *units[0].shape[1:]), BF16),
            pltpu.VMEM((tokens, wide_t), BF16),
            pltpu.VMEM((tokens, wide_s), BF16),
            pltpu.VMEM((tokens, columns), F32),
            pltpu.VMEM((64, 8, LANES), F32),
            pltpu.VMEM((tokens, LANES), F32),
            pltpu.SemaphoreType.DMA((2, 8)),
            pltpu.SemaphoreType.DMA((2,)),
        ],
        compiler_params=params(24),
        cost_estimate=cost(2 * tokens * (wide_t + wide_s) * columns, 8 << 20),
    )(place, *map(in_hbm, units), *map(in_vmem, (heads_t, heads_s)))


def gradient_of(place, lengths, stats, teacher, student, own_s, other_s):
    tokens, columns = teacher.shape
    wide = own_s.shape[0]
    return pl.pallas_call(
        gradient_kernel,
        name="hidden_gradient",
        in_specs=[SMEM] * 2 + [VMEM] * 3 + [HBM] * 2,
        out_specs=[HBM, HBM, VMEM],
        out_shape=[
            pltpu.HBM((8, 8, HALF, wide // 8), BF16),
            pltpu.HBM((tokens, columns), BF16),
            jax.ShapeDtypeStruct((8, tokens), F32),
        ],
        scratch_shapes=[
            pltpu.VMEM((wide, columns), BF16),
            pltpu.VMEM((8, 8, HALF, wide // 8), BF16),
            pltpu.VMEM((tokens, columns), BF16),
            pltpu.VMEM((tokens, LANES), F32),
            pltpu.SemaphoreType.DMA((8,)),
            pltpu.SemaphoreType.DMA((5,)),
        ],
        compiler_params=params(LIMIT),
        cost_estimate=cost(2 * tokens * wide * columns, 2 * wide * columns),
    )(place, lengths, *map(in_vmem, (stats, teacher, student)), *map(in_hbm, (own_s, other_s)))


def head_gradient_of(own, other, mine, got):
    (tokens, wide), columns = own.shape, got.shape[1]
    width = wide // 8
    strip = pl.BlockSpec((tokens, width), lambda k: (0, k))
    whole = pl.BlockSpec((tokens, columns), lambda k: (0, 0))
    return pl.pallas_call(
        head_kernel,
        name="head_gradient",
        grid=(8,),
        in_specs=[strip, strip, whole, whole],
        out_specs=pl.BlockSpec((width, columns), lambda k: (k, 0)),
        out_shape=jax.ShapeDtypeStruct((wide, columns), BF16),
        compiler_params=params(LIMIT),
        cost_estimate=cost(4 * tokens * wide * columns, 16 << 20),
    )(own, other, mine, got)


def pack_kernel(core_ref, own_t_in, got_t, own_s_in, got_s, ids_ref, out_ref, own_t, own_s, sems):
    copies = [
        pltpu.make_async_copy(own_t_in, own_t, sems.at[0]),
        pltpu.make_async_copy(own_s_in, own_s, sems.at[1]),
    ]
    for copy in copies:
        copy.start()
    first = core_ref[0] == 0

    def sides(own_ref, got_ref):
        own, got = (ref[...].astype(F32) for ref in (own_ref, got_ref))
        own, got = (jnp.where(first, v[:HALF], v[HALF:]) for v in (own, got))
        return jnp.where(first, own, got), jnp.where(first, got, own)

    ids = jnp.where(first, ids_ref[:, :HALF], ids_ref[:, HALF:])
    ids = jnp.concatenate([ids, jnp.zeros((1, LANES - HALF), jnp.int32)], axis=1)
    ids = jnp.concatenate([ids // 4096, ids // 64 % 64, ids % 64, jnp.zeros((ID_ROWS - 3, LANES), jnp.int32)], axis=0)
    for copy in copies:
        copy.wait()
    teacher = jnp.concatenate(sides(own_t, got_t), axis=1)
    student = jnp.concatenate(sides(own_s, got_s), axis=1)
    rows = [teacher[:, i : i + LANES] for i in range(0, teacher.shape[1], LANES)]
    rows.append(ids.astype(F32))
    rows += [student[:, i : i + LANES] for i in range(0, student.shape[1], LANES)]
    block = jnp.concatenate(rows, axis=0).astype(BF16)
    out_ref[...] = jnp.broadcast_to(block, out_ref.shape)


def pack(core, own_t, got_t, own_s, got_s, sampled):
    rows = (own_t.shape[1] + own_s.shape[1]) * 2 * HALF // LANES + ID_ROWS
    return pl.pallas_call(
        pack_kernel,
        name="pack",
        in_specs=[SMEM, HBM, VMEM, HBM, VMEM, VMEM],
        out_specs=VMEM,
        out_shape=jax.ShapeDtypeStruct((8, rows, LANES), BF16),
        scratch_shapes=[
            pltpu.VMEM(own_t.shape, BF16),
            pltpu.VMEM(own_s.shape, BF16),
            pltpu.SemaphoreType.DMA((2,)),
        ],
        compiler_params=params(6),
        cost_estimate=cost(0, 1 << 20),
    )(core.reshape(1).astype(jnp.int32), in_hbm(own_t), in_vmem(got_t), in_hbm(own_s), in_vmem(got_s), sampled.reshape(1, 2 * HALF))


def per_device(teacher_hidden, student_hidden, teacher_head, student_head, lengths, sampled):
    group, member = lax.axis_index("grp"), lax.axis_index("vocab")
    core = member % 2
    is_first = core == 0
    wide_t, columns = teacher_head.shape
    wide_s = student_head.shape[0]
    tokens = 8 * HALF
    part_t, part_s = wide_t // 8, wide_s // 8
    strips_t, strips_s = part_t // LANES, part_s // LANES

    got_t, got_s = swap(teacher_hidden), swap(student_hidden)
    teacher_late, student_late, got_t, got_s = lax.optimization_barrier((teacher_head, student_head, got_t, got_s))
    other_teacher_head = swap(teacher_late)
    other_student_head = swap(student_late)

    blocks = pack(core, teacher_hidden, got_t, student_hidden, got_s, sampled)
    near = lax.all_to_all(blocks, BOTH, 0, 0, axis_index_groups=FIRST)
    near, other_student_head = lax.optimization_barrier((near, other_student_head))
    units = second_gather(near)
    heads_t, heads_s = prefetch(
        teacher_head, other_teacher_head, student_head, other_student_head, units[1:4]
    )

    number_of = group * lax.axis_size("vocab") + member
    x_high, y, x_low, z = member // 8, member // 2 % 4, group // 4, group % 4
    corner = x_high * 4 + y // 2 * 2 + z // 2
    corner = corner ^ (core * (x_low * 4 + y % 2 * 2 + z % 2))
    place = [number_of * columns, (number_of + 1 - 2 * core) * columns, corner, core]
    place = jnp.stack(place).astype(jnp.int32)
    teacher_logits, student_logits, stats, own_rows = logits_of(place, units, heads_t, heads_s)
    other_rows = swap(own_rows)
    all_stats = lax.all_to_all(stats, BOTH, 0, 0, axis_index_groups=SAME_CORE)

    part, grads, kl = gradient_of(
        place, lengths, all_stats, teacher_logits, student_logits, student_head, other_student_head
    )
    got_grad = swap(grads[:, columns:])
    parts = lax.all_to_all(part.reshape(64, HALF, part_s), BOTH, 0, 0, axis_index_groups=SAME_CORE)
    head_grad = head_gradient_of(own_rows, other_rows, grads, got_grad)
    parts, head_grad = lax.optimization_barrier((parts, head_grad))
    hidden = jnp.sum(parts.astype(F32), axis=0).astype(BF16)
    one, two = hidden[:, : part_s // 2], hidden[:, part_s // 2 :]
    kept = jnp.where(is_first, one, two)
    got = swap(jnp.where(is_first, two, one))
    hidden_grad = jnp.concatenate(
        [jnp.where(is_first, kept, got), jnp.where(is_first, got, kept)], axis=0
    )

    def own_tokens(who):
        return lax.dynamic_slice(kl, (0, group * HALF + (4 * who) % HALF), (2, 4))

    got = swap(own_tokens(member + 1 - 2 * core))
    out = jnp.where(member // 8 == core, own_tokens(member), got)
    return head_grad, hidden_grad, out[0], out[1]


def solution(mesh):
    return jax.shard_map(
        per_device,
        mesh=mesh,
        in_specs=(
            P("grp", "vocab"),
            P("grp", "vocab"),
            P(None, BOTH),
            P(None, BOTH),
            P(),
            P("grp"),
        ),
        out_specs=(P(None, BOTH), P("grp", "vocab"), P(BOTH), P(BOTH)),
        check_vma=False,
    )
```

```python
import functools
import itertools

import jax
import jax.numpy as jnp
import numpy as np
from jax import lax
from jax.experimental import pallas as pl
from jax.experimental.pallas import tpu as pltpu
from jax.sharding import PartitionSpec as P

LOSS_SCALE = 16
BOTH = ("grp", "vocab")
F32, BF16 = jnp.float32, jnp.bfloat16
HALF = 32
LANES = 128
ID_ROWS = 16
PIECES = 2
LIMIT = 56
DEPTH = 8
TILE = 256
SHARES = ((), (0, 1), (2, 3), (4, 5), (6, 7))
CORNER_OF = (0, 4, 2, 1, 3, 5, 6, 7)


def device(x, y, z, core):
    return ((x % 2) * 4 + z) * 16 + ((x // 2) * 4 + y) * 2 + core


def cubes(core, step, rank):
    seen, groups = set(), []
    for where in itertools.product(range(4), repeat=3):
        if where in seen:
            continue
        pairs = [sorted((p, p ^ step), key=rank) for p in where]
        members = list(itertools.product(*pairs))
        seen.update(members)
        groups.append([device(*m, core) for m in members])
    return groups


def low(p):
    return p & 1


def high(p):
    return p >> 1


def parity(p):
    return (p & 1) ^ (p >> 1)


FIRST = cubes(0, 1, low) + cubes(1, 3, high)
SECOND = cubes(0, 3, high) + cubes(1, 1, parity)
SAME_CORE = [[2 * chip + core for chip in range(64)] for core in (0, 1)]
SWAP = [(i, i ^ 1) for i in range(128)]


def chips():
    return itertools.product(range(4), repeat=3)


def number(rank, place):
    return rank(place[0]) * 4 + rank(place[1]) * 2 + rank(place[2])


def positions():
    table = np.zeros((2, 64), np.int32)
    for place in chips():
        chip = device(*place, 0) // 2
        table[0, chip] = number(high, place) * 8 + number(low, place)
        table[1, chip] = number(parity, place) * 8 + number(high, place)
    return table


def links(axes):
    pairs = []
    for place in chips():
        for core in (0, 1):
            other = list(place)
            for axis in axes:
                other[axis] ^= (3, 1)[core]
            pairs.append((device(*place, core), device(*other, core)))
    return pairs


POSITIONS = positions()


def swap(value):
    return lax.ppermute(value, BOTH, SWAP)


def to_all(block, groups):
    size = len(groups[0])
    return lax.all_to_all(
        jnp.broadcast_to(block, (size,) + block.shape), BOTH, 0, 0, axis_index_groups=groups
    )


def second_gather(near):
    def along(value, *axes):
        return lax.ppermute(value, BOTH, links(axes))

    one = [along(near, axis) for axis in range(3)]
    far = along(near, 0, 1, 2)
    two = [along(one[(axis + 2) % 3], (axis + 1) % 3) for axis in range(3)]
    return [near, *one, *two, far]


def rows_of(core, blocks_ref, chunk, at, strips):
    parts = [blocks_ref[position(core, group, chunk), at : at + strips * HALF] for group in range(8)]
    return jnp.concatenate(
        [
            jnp.concatenate([p[s * HALF : (s + 1) * HALF] for p in parts], axis=0)
            for s in range(strips)
        ],
        axis=1,
    )


def position(core, group, chunk):
    zero, one = (int(table[group * 8 + chunk]) for table in POSITIONS)
    return zero + core * (one - zero)


class Stream:
    def __init__(self, sems):
        self.sems = sems
        self.copies = []
        self.started = 0

    def add(self, source, target):
        self.copies.append(pltpu.make_async_copy(source, target, self.sems.at[len(self.copies)]))
        return len(self.copies) - 1

    def start(self, count):
        for copy in self.copies[self.started : count]:
            copy.start()
        self.started = max(self.started, min(count, len(self.copies)))

    def wait(self, i):
        self.copies[i].wait()
        self.start(i + 1 + DEPTH)


def put_beside(pairs_and_buffers, sems):
    copies = []
    for pair, buffer in pairs_and_buffers:
        rows, columns = pair[0].shape
        size = rows // 4
        for i in range(4):
            for j, ref in enumerate(pair):
                at = pl.ds(i * size, size)
                copies.append(
                    pltpu.make_async_copy(
                        ref.at[at], buffer.at[at, pl.ds(j * columns, columns)], sems.at[len(copies)]
                    )
                )
                copies[-1].start()
    for copy in copies:
        copy.wait()


def prefetch_kernel(own_t, other_t, own_s, other_s, first, second, third, heads_t, heads_s, sems):
    put_beside([((own_t, other_t), heads_t), ((own_s, other_s), heads_s)], sems)


def logits_kernel(
    place_ref, *refs
):
    units, (heads_t, heads_s, teacher, student, stats_out, lhs_out) = refs[:8], refs[8:14]
    blocks_ref, lhs_t, lhs_s, powers, stats, work, sems, out_sems = refs[14:]
    core = place_ref[3]
    at_s = 4 * HALF + ID_ROWS
    arriving = []
    for part, (at, size) in enumerate(((0, at_s), (at_s, 5 * HALF))):
        for n, unit in enumerate(units):
            start = (place_ref[2] ^ CORNER_OF[n]) * 8
            rows = pl.ds(at, size)
            arriving.append(
                pltpu.make_async_copy(
                    unit.at[:, rows], blocks_ref.at[pl.ds(start, 8), rows], sems.at[part, n]
                )
            )
    for copy in arriving[:8]:
        copy.start()
    columns = heads_t.shape[1] // 2
    lane = lax.broadcasted_iota(jnp.int32, (HALF, LANES), 1)
    column = lax.broadcasted_iota(jnp.int32, (HALF, columns), 1)
    column = jnp.concatenate([column + place_ref[0], column + place_ref[1]], axis=1)

    def columns_of(values, first):
        row = jnp.zeros((HALF, LANES), F32)
        for j, value in enumerate(values):
            row = jnp.where(lane == first + j, value, row)
        return row

    def teacher_values(group):
        rows = pl.ds(group * HALF, HALF)
        t = teacher[rows, :]
        top = jnp.max(t, axis=1, keepdims=True)
        t = t - top
        e = jnp.exp(t)
        powers[rows, :] = e
        work[rows, :] = columns_of(
            (top, jnp.sum(e, axis=1, keepdims=True), jnp.sum(e * t, axis=1, keepdims=True)), 0
        )

    for copy in arriving[:8]:
        copy.wait()
    for copy in arriving[8:]:
        copy.start()
    for chunk in range(8):
        lhs_t[:, chunk * 4 * LANES : (chunk + 1) * 4 * LANES] = rows_of(core, blocks_ref, chunk, 0, 4)
    for j, chunks in enumerate(SHARES):
        at = slice(j * TILE, (j + 1) * TILE)
        teacher[:, at] = jnp.dot(lhs_t[...], heads_t[:, at], preferred_element_type=F32)
        if j == 1:
            for copy in arriving[8:]:
                copy.wait()
        for chunk in chunks:
            lhs_s[:, chunk * 5 * LANES : (chunk + 1) * 5 * LANES] = rows_of(
                core, blocks_ref, chunk, at_s, 5
            )
    leaving = [pltpu.make_async_copy(lhs_s, lhs_out, out_sems.at[0])]
    leaving[0].start()
    for j, groups in enumerate(SHARES):
        at = slice(j * TILE, (j + 1) * TILE)
        student[:, at] = jnp.dot(lhs_s[...], heads_s[:, at], preferred_element_type=F32)
        for group in groups:
            teacher_values(group)
    digits = [blocks_ref[position(core, group, 0), 4 * HALF : at_s].astype(F32) for group in range(8)]
    ids = jnp.concatenate([d[0:1] * 4096.0 + d[1:2] * 64.0 + d[2:3] for d in digits], axis=0)
    ids = jnp.concatenate([ids, jnp.zeros((LANES - 8, LANES), F32)], axis=0).T.astype(jnp.int32)
    for group in range(8):
        rows = pl.ds(group * HALF, HALF)
        s = student[rows, :]
        hit = column == ids[:HALF, group : group + 1]
        picked = jnp.sum(jnp.where(hit, teacher[rows, :] - s, 0.0), axis=1, keepdims=True)
        top = jnp.max(s, axis=1, keepdims=True)
        s = s - top
        log_s = jnp.log(jnp.sum(jnp.exp(s), axis=1, keepdims=True))
        term = jnp.sum(powers[rows, :] * s, axis=1, keepdims=True)
        top_t, sum_t, term_t = (work[rows, j : j + 1] for j in range(3))
        log_t = jnp.log(sum_t)
        ratio = (term_t - term) / sum_t - (log_t - log_s)
        work[rows, :] = columns_of((top_t + log_t, top + log_s, ratio, picked), 0)
    values = work[...].T
    values = [values[j : j + 1, h * LANES : (h + 1) * LANES] for j in range(4) for h in range(2)]
    stats[...] = jnp.broadcast_to(jnp.concatenate(values, axis=0), stats.shape)
    leaving.append(pltpu.make_async_copy(stats, stats_out, out_sems.at[1]))
    leaving[1].start()
    for copy in leaving:
        copy.wait()


def gradient_kernel(
    place_ref, lengths_ref, stats_ref, teacher, student, own_s, other_s, part_out, grads_out, kl_ref,
    heads, part, grads, work, sems, out_sems,
):
    stream = Stream(sems)
    size, columns = own_s.shape[0] // 4, own_s.shape[1]
    for i in range(4):
        at = pl.ds(i * size, size)
        for j, ref in enumerate((own_s, other_s)):
            stream.add(ref.at[at], heads.at[at, pl.ds(j * columns, columns)])
    stream.start(DEPTH)
    part_t, part_s, ratios, picked = (stats_ref[:, 2 * j : 2 * j + 2, :] for j in range(4))

    def log_sum(parts):
        top = jnp.max(parts, axis=0, keepdims=True)
        return top + jnp.log(jnp.sum(jnp.exp(parts - top), axis=0, keepdims=True))

    lse_t, lse_s = log_sum(part_t), log_sum(part_s)
    from_t = part_t - lse_t
    kl = jnp.sum(jnp.exp(from_t) * (ratios + (from_t - (part_s - lse_s))), axis=0)
    lse_t, lse_s = lse_t[0], lse_s[0]
    ratio = jnp.sum(picked, axis=0) - (lse_t - lse_s)

    def row(value):
        return jnp.concatenate([value[0:1], value[1:2]], axis=1)

    tokens = 2 * LANES
    kl_ref[...] = jnp.concatenate([row(kl), row(ratio), jnp.zeros((6, tokens), F32)], axis=0)
    token = lax.broadcasted_iota(jnp.int32, (1, tokens), 1)
    token = token + (token // HALF + place_ref[3]) * HALF
    length, end = jnp.zeros((1, tokens), jnp.int32), jnp.int32(0)
    for i in range(lengths_ref.shape[0]):
        inside = token >= end
        end = end + lengths_ref[i]
        length = jnp.where(inside & (token < end), lengths_ref[i], length)
    weight = (LOSS_SCALE * 2 * tokens / lengths_ref.shape[0]) / length.astype(F32)
    rows = jnp.concatenate([row(lse_t), row(lse_s), weight, jnp.zeros((LANES - 3, tokens), F32)], axis=0)
    work[...] = rows.T

    for i in range(tokens // HALF):
        at = pl.ds(i * HALF, HALF)
        at_t, at_s, weight = (work[at, j : j + 1] for j in range(3))
        grad = weight * (jnp.exp(student[at, :] - at_s) - jnp.exp(teacher[at, :] - at_t))
        grads[at, :] = grad.astype(BF16)
    leaving = [pltpu.make_async_copy(grads, grads_out, out_sems.at[64])]
    leaving[0].start()
    width = part.shape[2]
    chunks = size // width
    for i in range(4):
        stream.wait(2 * i)
        stream.wait(2 * i + 1)
        product = lax.dot_general(
            grads[...], heads[i * size : (i + 1) * size, :], (((1,), (1,)), ((), ())), preferred_element_type=F32
        ).astype(BF16)
        for group in range(8):
            for j in range(chunks):
                chunk = chunks * i + j
                to = position(place_ref[3], group, chunk)
                part[to] = product[group * HALF : (group + 1) * HALF, j * width : (j + 1) * width]
                leaving.append(
                    pltpu.make_async_copy(part.at[to], part_out.at[to], out_sems.at[group * 8 + chunk])
                )
                leaving[-1].start()
    for copy in leaving:
        copy.wait()


def head_kernel(own_ref, other_ref, mine_ref, got_ref, out_ref):
    rows = jnp.concatenate([own_ref[...], other_ref[...]], axis=0)
    grad = jnp.concatenate([mine_ref[...], got_ref[...]], axis=0)
    out_ref[...] = lax.dot_general(
        rows, grad, (((0,), (0,)), ((), ())), preferred_element_type=F32
    ).astype(BF16)


SMEM = pl.BlockSpec(memory_space=pltpu.SMEM)
VMEM = pl.BlockSpec(memory_space=pltpu.VMEM)
HBM = pl.BlockSpec(memory_space=pltpu.HBM)


def in_hbm(value):
    return pltpu.with_memory_space_constraint(value, pltpu.HBM)


def params(limit):
    return pltpu.CompilerParams(vmem_limit_bytes=limit << 20)


def cost(flops, size):
    return pl.CostEstimate(flops=flops, bytes_accessed=size, transcendentals=0)


def in_vmem(value):
    return pltpu.with_memory_space_constraint(value, pltpu.VMEM)


def prefetch(own_t, other_t, own_s, other_s, after):
    (wide_t, columns), wide_s = own_t.shape, own_s.shape[0]
    return pl.pallas_call(
        prefetch_kernel,
        name="prefetch_heads",
        in_specs=[HBM] * 4 + [pl.BlockSpec(memory_space=pl.ANY)] * len(after),
        out_specs=[VMEM] * 2,
        out_shape=[pltpu.VMEM((wide_t, 2 * columns), BF16), pltpu.VMEM((wide_s, 2 * columns), BF16)],
        scratch_shapes=[pltpu.SemaphoreType.DMA((16,))],
        compiler_params=params(2),
        cost_estimate=cost(0, 8 * (wide_t + wide_s) * columns),
    )(*map(in_hbm, (own_t, other_t, own_s, other_s)), *after)


def logits_of(place, units, heads_t, heads_s):
    tokens = 8 * HALF
    (wide_t, columns), wide_s = heads_t.shape, heads_s.shape[0]
    logits = pltpu.VMEM((tokens, columns), F32)
    return pl.pallas_call(
        logits_kernel,
        name="logits",
        in_specs=[SMEM] + [HBM] * 8 + [VMEM] * 2,
        out_specs=[VMEM, VMEM, HBM, HBM],
        out_shape=[
            logits,
            logits,
            pltpu.HBM((64, 8, LANES), F32),
            pltpu.HBM((tokens, wide_s), BF16),
        ],
        scratch_shapes=[
            pltpu.VMEM((64, *units[0].shape[1:]), BF16),
            pltpu.VMEM((tokens, wide_t), BF16),
            pltpu.VMEM((tokens, wide_s), BF16),
            pltpu.VMEM((tokens, columns), F32),
            pltpu.VMEM((64, 8, LANES), F32),
            pltpu.VMEM((tokens, LANES), F32),
            pltpu.SemaphoreType.DMA((2, 8)),
            pltpu.SemaphoreType.DMA((2,)),
        ],
        compiler_params=params(24),
        cost_estimate=cost(2 * tokens * (wide_t + wide_s) * columns, 8 << 20),
    )(place, *map(in_hbm, units), *map(in_vmem, (heads_t, heads_s)))


def gradient_of(place, lengths, stats, teacher, student, own_s, other_s):
    tokens, columns = teacher.shape
    wide = own_s.shape[0]
    return pl.pallas_call(
        gradient_kernel,
        name="hidden_gradient",
        in_specs=[SMEM] * 2 + [VMEM] * 3 + [HBM] * 2,
        out_specs=[HBM, HBM, VMEM],
        out_shape=[
            pltpu.HBM((64, HALF, wide // 8), BF16),
            pltpu.HBM((tokens, columns), BF16),
            jax.ShapeDtypeStruct((8, tokens), F32),
        ],
        scratch_shapes=[
            pltpu.VMEM((wide, columns), BF16),
            pltpu.VMEM((64, HALF, wide // 8), BF16),
            pltpu.VMEM((tokens, columns), BF16),
            pltpu.VMEM((tokens, LANES), F32),
            pltpu.SemaphoreType.DMA((8,)),
            pltpu.SemaphoreType.DMA((65,)),
        ],
        compiler_params=params(LIMIT),
        cost_estimate=cost(2 * tokens * wide * columns, 2 * wide * columns),
    )(place, lengths, *map(in_vmem, (stats, teacher, student)), *map(in_hbm, (own_s, other_s)))


def head_gradient_of(own, other, mine, got):
    (tokens, wide), columns = own.shape, got.shape[1]
    width = wide // 8
    strip = pl.BlockSpec((tokens, width), lambda k: (0, k))
    whole = pl.BlockSpec((tokens, columns), lambda k: (0, 0))
    return pl.pallas_call(
        head_kernel,
        name="head_gradient",
        grid=(8,),
        in_specs=[strip, strip, whole, whole],
        out_specs=pl.BlockSpec((width, columns), lambda k: (k, 0)),
        out_shape=jax.ShapeDtypeStruct((wide, columns), BF16),
        compiler_params=params(LIMIT),
        cost_estimate=cost(4 * tokens * wide * columns, 16 << 20),
    )(own, other, mine, got)


def pack_kernel(core_ref, own_t_in, got_t, own_s_in, got_s, ids_ref, out_ref, own_t, own_s, sems):
    copies = [
        pltpu.make_async_copy(own_t_in, own_t, sems.at[0]),
        pltpu.make_async_copy(own_s_in, own_s, sems.at[1]),
    ]
    for copy in copies:
        copy.start()
    first = core_ref[0] == 0

    def sides(own_ref, got_ref):
        own, got = (ref[...].astype(F32) for ref in (own_ref, got_ref))
        own, got = (jnp.where(first, v[:HALF], v[HALF:]) for v in (own, got))
        return jnp.where(first, own, got), jnp.where(first, got, own)

    ids = jnp.where(first, ids_ref[:, :HALF], ids_ref[:, HALF:])
    ids = jnp.concatenate([ids, jnp.zeros((1, LANES - HALF), jnp.int32)], axis=1)
    ids = jnp.concatenate([ids // 4096, ids // 64 % 64, ids % 64, jnp.zeros((ID_ROWS - 3, LANES), jnp.int32)], axis=0)
    for copy in copies:
        copy.wait()
    teacher = jnp.concatenate(sides(own_t, got_t), axis=1)
    student = jnp.concatenate(sides(own_s, got_s), axis=1)
    rows = [teacher[:, i : i + LANES] for i in range(0, teacher.shape[1], LANES)]
    rows.append(ids.astype(F32))
    rows += [student[:, i : i + LANES] for i in range(0, student.shape[1], LANES)]
    block = jnp.concatenate(rows, axis=0).astype(BF16)
    out_ref[...] = jnp.broadcast_to(block, out_ref.shape)


def pack(core, own_t, got_t, own_s, got_s, sampled):
    rows = (own_t.shape[1] + own_s.shape[1]) * 2 * HALF // LANES + ID_ROWS
    return pl.pallas_call(
        pack_kernel,
        name="pack",
        in_specs=[SMEM, HBM, VMEM, HBM, VMEM, VMEM],
        out_specs=VMEM,
        out_shape=jax.ShapeDtypeStruct((8, rows, LANES), BF16),
        scratch_shapes=[
            pltpu.VMEM(own_t.shape, BF16),
            pltpu.VMEM(own_s.shape, BF16),
            pltpu.SemaphoreType.DMA((2,)),
        ],
        compiler_params=params(6),
        cost_estimate=cost(0, 1 << 20),
    )(core.reshape(1).astype(jnp.int32), in_hbm(own_t), in_vmem(got_t), in_hbm(own_s), in_vmem(got_s), sampled.reshape(1, 2 * HALF))


def per_device(teacher_hidden, student_hidden, teacher_head, student_head, lengths, sampled):
    group, member = lax.axis_index("grp"), lax.axis_index("vocab")
    core = member % 2
    is_first = core == 0
    wide_t, columns = teacher_head.shape
    wide_s = student_head.shape[0]
    tokens = 8 * HALF
    part_t, part_s = wide_t // 8, wide_s // 8
    strips_t, strips_s = part_t // LANES, part_s // LANES

    got_t, got_s = swap(teacher_hidden), swap(student_hidden)
    teacher_late, student_late, got_t, got_s = lax.optimization_barrier((teacher_head, student_head, got_t, got_s))
    other_teacher_head = swap(teacher_late)
    other_student_head = swap(student_late)

    blocks = pack(core, teacher_hidden, got_t, student_hidden, got_s, sampled)
    near = lax.all_to_all(blocks, BOTH, 0, 0, axis_index_groups=FIRST)
    near, other_student_head = lax.optimization_barrier((near, other_student_head))
    units = second_gather(near)
    heads_t, heads_s = prefetch(
        teacher_head, other_teacher_head, student_head, other_student_head, units[1:4]
    )

    number_of = group * lax.axis_size("vocab") + member
    x_high, y, x_low, z = member // 8, member // 2 % 4, group // 4, group % 4
    corner = x_high * 4 + y // 2 * 2 + z // 2
    corner = corner ^ (core * (x_low * 4 + y % 2 * 2 + z % 2))
    place = [number_of * columns, (number_of + 1 - 2 * core) * columns, corner, core]
    place = jnp.stack(place).astype(jnp.int32)
    teacher_logits, student_logits, stats, own_rows = logits_of(place, units, heads_t, heads_s)
    all_stats = lax.all_to_all(stats, BOTH, 0, 0, axis_index_groups=SAME_CORE)

    part, grads, kl = gradient_of(
        place, lengths, all_stats, teacher_logits, student_logits, student_head, other_student_head
    )
    grads, late_rows = lax.optimization_barrier((grads, own_rows))
    other_rows = swap(late_rows)
    got_grad = swap(grads[:, columns:])

    def spread(value, groups):
        return lax.all_to_all(value, BOTH, 0, 0, axis_index_groups=groups)

    parts = spread(part.reshape(8, 8, HALF, part_s), SECOND)
    head_grad = head_gradient_of(own_rows, other_rows, grads, got_grad)
    parts, head_grad = lax.optimization_barrier((parts, head_grad))
    parts = spread(jnp.sum(parts.astype(F32), axis=0).astype(BF16), FIRST)
    hidden = jnp.sum(parts.astype(F32), axis=0).astype(BF16)
    one, two = hidden[:, : part_s // 2], hidden[:, part_s // 2 :]
    kept = jnp.where(is_first, one, two)
    got = swap(jnp.where(is_first, two, one))
    hidden_grad = jnp.concatenate(
        [jnp.where(is_first, kept, got), jnp.where(is_first, got, kept)], axis=0
    )

    def own_tokens(who):
        return lax.dynamic_slice(kl, (0, group * HALF + (4 * who) % HALF), (2, 4))

    got = swap(own_tokens(member + 1 - 2 * core))
    out = jnp.where(member // 8 == core, own_tokens(member), got)
    return head_grad, hidden_grad, out[0], out[1]


def solution(mesh):
    return jax.shard_map(
        per_device,
        mesh=mesh,
        in_specs=(
            P("grp", "vocab"),
            P("grp", "vocab"),
            P(None, BOTH),
            P(None, BOTH),
            P(),
            P("grp"),
        ),
        out_specs=(P(None, BOTH), P("grp", "vocab"), P(BOTH), P(BOTH)),
        check_vma=False,
    )
```

```python
import functools
import itertools

import jax
import jax.numpy as jnp
import numpy as np
from jax import lax
from jax.experimental import pallas as pl
from jax.experimental.pallas import tpu as pltpu
from jax.sharding import PartitionSpec as P

LOSS_SCALE = 16
BOTH = ("grp", "vocab")
F32, BF16 = jnp.float32, jnp.bfloat16
HALF = 32
LANES = 128
ID_ROWS = 16
PIECES = 2
LIMIT = 56
DEPTH = 8
TILE = 256
SHARES = ((), (0, 1), (2, 3), (4, 5), (6, 7))
CORNER_OF = (0, 4, 2, 1, 3, 5, 6, 7)


def device(x, y, z, core):
    return ((x % 2) * 4 + z) * 16 + ((x // 2) * 4 + y) * 2 + core


def cubes(core, step, rank):
    seen, groups = set(), []
    for where in itertools.product(range(4), repeat=3):
        if where in seen:
            continue
        pairs = [sorted((p, p ^ step), key=rank) for p in where]
        members = list(itertools.product(*pairs))
        seen.update(members)
        groups.append([device(*m, core) for m in members])
    return groups


def low(p):
    return p & 1


def high(p):
    return p >> 1


def parity(p):
    return (p & 1) ^ (p >> 1)


FIRST = cubes(0, 1, low) + cubes(1, 3, high)
SECOND = cubes(0, 3, high) + cubes(1, 1, parity)
SAME_CORE = [[2 * chip + core for chip in range(64)] for core in (0, 1)]
SWAP = [(i, i ^ 1) for i in range(128)]


def chips():
    return itertools.product(range(4), repeat=3)


def number(rank, place):
    return rank(place[0]) * 4 + rank(place[1]) * 2 + rank(place[2])


def positions():
    table = np.zeros((2, 64), np.int32)
    for place in chips():
        chip = device(*place, 0) // 2
        table[0, chip] = number(high, place) * 8 + number(low, place)
        table[1, chip] = number(parity, place) * 8 + number(high, place)
    return table


def links(axes):
    pairs = []
    for place in chips():
        for core in (0, 1):
            other = list(place)
            for axis in axes:
                other[axis] ^= (3, 1)[core]
            pairs.append((device(*place, core), device(*other, core)))
    return pairs


POSITIONS = positions()


def swap(value):
    return lax.ppermute(value, BOTH, SWAP)


def to_all(block, groups):
    size = len(groups[0])
    return lax.all_to_all(
        jnp.broadcast_to(block, (size,) + block.shape), BOTH, 0, 0, axis_index_groups=groups
    )


def second_gather(near):
    def along(value, *axes):
        return lax.ppermute(value, BOTH, links(axes))

    one = [along(near, axis) for axis in range(3)]
    far = along(near, 0, 1, 2)
    two = [along(one[(axis + 2) % 3], (axis + 1) % 3) for axis in range(3)]
    return [near, *one, *two, far]


def rows_of(core, blocks_ref, chunk, at, strips):
    parts = [blocks_ref[position(core, group, chunk), at : at + strips * HALF] for group in range(8)]
    return jnp.concatenate(
        [
            jnp.concatenate([p[s * HALF : (s + 1) * HALF] for p in parts], axis=0)
            for s in range(strips)
        ],
        axis=1,
    )


def position(core, group, chunk):
    zero, one = (int(table[group * 8 + chunk]) for table in POSITIONS)
    return zero + core * (one - zero)


class Stream:
    def __init__(self, sems):
        self.sems = sems
        self.copies = []
        self.started = 0

    def add(self, source, target):
        self.copies.append(pltpu.make_async_copy(source, target, self.sems.at[len(self.copies)]))
        return len(self.copies) - 1

    def start(self, count):
        for copy in self.copies[self.started : count]:
            copy.start()
        self.started = max(self.started, min(count, len(self.copies)))

    def wait(self, i):
        self.copies[i].wait()
        self.start(i + 1 + DEPTH)


def put_beside(pairs_and_buffers, sems):
    copies = []
    for pair, buffer in pairs_and_buffers:
        rows, columns = pair[0].shape
        size = rows // 4
        for i in range(4):
            for j, ref in enumerate(pair):
                at = pl.ds(i * size, size)
                copies.append(
                    pltpu.make_async_copy(
                        ref.at[at], buffer.at[at, pl.ds(j * columns, columns)], sems.at[len(copies)]
                    )
                )
                copies[-1].start()
    for copy in copies:
        copy.wait()


def prefetch_kernel(own_t, other_t, own_s, other_s, first, second, third, heads_t, heads_s, sems):
    put_beside([((own_t, other_t), heads_t), ((own_s, other_s), heads_s)], sems)


def logits_kernel(
    place_ref, *refs
):
    units, (heads_t, heads_s, teacher, student, stats_out, lhs_out) = refs[:8], refs[8:14]
    blocks_ref, lhs_t, lhs_s, powers, stats, work, sems, out_sems = refs[14:]
    core = place_ref[3]
    at_s = 4 * HALF + ID_ROWS
    arriving = []
    for part, (at, size) in enumerate(((0, at_s), (at_s, 5 * HALF))):
        for n, unit in enumerate(units):
            start = (place_ref[2] ^ CORNER_OF[n]) * 8
            rows = pl.ds(at, size)
            arriving.append(
                pltpu.make_async_copy(
                    unit.at[:, rows], blocks_ref.at[pl.ds(start, 8), rows], sems.at[part, n]
                )
            )
    for copy in arriving[:8]:
        copy.start()
    columns = heads_t.shape[1] // 2
    lane = lax.broadcasted_iota(jnp.int32, (HALF, LANES), 1)
    column = lax.broadcasted_iota(jnp.int32, (HALF, columns), 1)
    column = jnp.concatenate([column + place_ref[0], column + place_ref[1]], axis=1)

    def columns_of(values, first):
        row = jnp.zeros((HALF, LANES), F32)
        for j, value in enumerate(values):
            row = jnp.where(lane == first + j, value, row)
        return row

    def teacher_values(group):
        rows = pl.ds(group * HALF, HALF)
        t = teacher[rows, :]
        top = jnp.max(t, axis=1, keepdims=True)
        t = t - top
        e = jnp.exp(t)
        powers[rows, :] = e
        work[rows, :] = columns_of(
            (top, jnp.sum(e, axis=1, keepdims=True), jnp.sum(e * t, axis=1, keepdims=True)), 0
        )

    for copy in arriving[:8]:
        copy.wait()
    for copy in arriving[8:]:
        copy.start()
    for chunk in range(8):
        lhs_t[:, chunk * 4 * LANES : (chunk + 1) * 4 * LANES] = rows_of(core, blocks_ref, chunk, 0, 4)
    for j, chunks in enumerate(SHARES):
        at = slice(j * TILE, (j + 1) * TILE)
        teacher[:, at] = jnp.dot(lhs_t[...], heads_t[:, at], preferred_element_type=F32)
        if j == 1:
            for copy in arriving[8:]:
                copy.wait()
        for chunk in chunks:
            lhs_s[:, chunk * 5 * LANES : (chunk + 1) * 5 * LANES] = rows_of(
                core, blocks_ref, chunk, at_s, 5
            )
    leaving = [pltpu.make_async_copy(lhs_s, lhs_out, out_sems.at[0])]
    leaving[0].start()
    for j, groups in enumerate(SHARES):
        at = slice(j * TILE, (j + 1) * TILE)
        student[:, at] = jnp.dot(lhs_s[...], heads_s[:, at], preferred_element_type=F32)
        for group in groups:
            teacher_values(group)
    digits = [blocks_ref[position(core, group, 0), 4 * HALF : at_s].astype(F32) for group in range(8)]
    ids = jnp.concatenate([d[0:1] * 4096.0 + d[1:2] * 64.0 + d[2:3] for d in digits], axis=0)
    ids = jnp.concatenate([ids, jnp.zeros((LANES - 8, LANES), F32)], axis=0).T.astype(jnp.int32)
    for group in range(8):
        rows = pl.ds(group * HALF, HALF)
        s = student[rows, :]
        hit = column == ids[:HALF, group : group + 1]
        picked = jnp.sum(jnp.where(hit, teacher[rows, :] - s, 0.0), axis=1, keepdims=True)
        top = jnp.max(s, axis=1, keepdims=True)
        s = s - top
        log_s = jnp.log(jnp.sum(jnp.exp(s), axis=1, keepdims=True))
        term = jnp.sum(powers[rows, :] * s, axis=1, keepdims=True)
        top_t, sum_t, term_t = (work[rows, j : j + 1] for j in range(3))
        log_t = jnp.log(sum_t)
        ratio = (term_t - term) / sum_t - (log_t - log_s)
        work[rows, :] = columns_of((top_t + log_t, top + log_s, ratio, picked), 0)
    values = work[...].T
    values = [values[j : j + 1, h * LANES : (h + 1) * LANES] for j in range(4) for h in range(2)]
    stats[...] = jnp.broadcast_to(jnp.concatenate(values, axis=0), stats.shape)
    leaving.append(pltpu.make_async_copy(stats, stats_out, out_sems.at[1]))
    leaving[1].start()
    for copy in leaving:
        copy.wait()


def gradient_kernel(
    place_ref, lengths_ref, stats_ref, teacher, student, own_s, other_s, part_out, grads_out, kl_ref,
    heads, part, grads, work, sems, out_sems,
):
    stream = Stream(sems)
    size, columns = own_s.shape[0] // 4, own_s.shape[1]
    for i in range(4):
        at = pl.ds(i * size, size)
        for j, ref in enumerate((own_s, other_s)):
            stream.add(ref.at[at], heads.at[at, pl.ds(j * columns, columns)])
    stream.start(DEPTH)
    part_t, part_s, ratios, picked = (stats_ref[:, 2 * j : 2 * j + 2, :] for j in range(4))

    def log_sum(parts):
        top = jnp.max(parts, axis=0, keepdims=True)
        return top + jnp.log(jnp.sum(jnp.exp(parts - top), axis=0, keepdims=True))

    lse_t, lse_s = log_sum(part_t), log_sum(part_s)
    from_t = part_t - lse_t
    kl = jnp.sum(jnp.exp(from_t) * (ratios + (from_t - (part_s - lse_s))), axis=0)
    lse_t, lse_s = lse_t[0], lse_s[0]
    ratio = jnp.sum(picked, axis=0) - (lse_t - lse_s)

    def row(value):
        return jnp.concatenate([value[0:1], value[1:2]], axis=1)

    tokens = 2 * LANES
    kl_ref[...] = jnp.concatenate([row(kl), row(ratio), jnp.zeros((6, tokens), F32)], axis=0)
    token = lax.broadcasted_iota(jnp.int32, (1, tokens), 1)
    token = token + (token // HALF + place_ref[3]) * HALF
    length, end = jnp.zeros((1, tokens), jnp.int32), jnp.int32(0)
    for i in range(lengths_ref.shape[0]):
        inside = token >= end
        end = end + lengths_ref[i]
        length = jnp.where(inside & (token < end), lengths_ref[i], length)
    weight = (LOSS_SCALE * 2 * tokens / lengths_ref.shape[0]) / length.astype(F32)
    rows = jnp.concatenate([row(lse_t), row(lse_s), weight, jnp.zeros((LANES - 3, tokens), F32)], axis=0)
    work[...] = rows.T

    for i in range(tokens // HALF):
        at = pl.ds(i * HALF, HALF)
        at_t, at_s, weight = (work[at, j : j + 1] for j in range(3))
        grad = weight * (jnp.exp(student[at, :] - at_s) - jnp.exp(teacher[at, :] - at_t))
        grads[at, :] = grad.astype(BF16)
    leaving = [pltpu.make_async_copy(grads, grads_out, out_sems.at[4])]
    leaving[0].start()
    width = part.shape[3]
    chunks = size // width
    core = place_ref[3]

    def piece(i, who):
        at = (pl.ds(2 * i, 2),) if who == 0 else (slice(None), pl.ds(2 * i, 2))
        return pltpu.make_async_copy(part.at[at], part_out.at[at], out_sems.at[i])

    def by_core(act):
        for who in (0, 1):
            pl.when(core == who)(lambda who=who: act(who))

    for i in range(4):
        stream.wait(2 * i)
        stream.wait(2 * i + 1)
        product = lax.dot_general(
            grads[...], heads[i * size : (i + 1) * size, :], (((1,), (1,)), ((), ())), preferred_element_type=F32
        ).astype(BF16)
        for group in range(8):
            for j in range(chunks):
                to = position(core, group, chunks * i + j)
                part[to // 8, to % 8] = product[group * HALF : (group + 1) * HALF, j * width : (j + 1) * width]
        by_core(lambda who, i=i: piece(i, who).start())
    by_core(lambda who: [piece(i, who).wait() for i in range(4)] and None)
    for copy in leaving:
        copy.wait()


def head_kernel(own_ref, other_ref, mine_ref, got_ref, out_ref):
    rows = jnp.concatenate([own_ref[...], other_ref[...]], axis=0)
    grad = jnp.concatenate([mine_ref[...], got_ref[...]], axis=0)
    out_ref[...] = lax.dot_general(
        rows, grad, (((0,), (0,)), ((), ())), preferred_element_type=F32
    ).astype(BF16)


SMEM = pl.BlockSpec(memory_space=pltpu.SMEM)
VMEM = pl.BlockSpec(memory_space=pltpu.VMEM)
HBM = pl.BlockSpec(memory_space=pltpu.HBM)


def in_hbm(value):
    return pltpu.with_memory_space_constraint(value, pltpu.HBM)


def params(limit):
    return pltpu.CompilerParams(vmem_limit_bytes=limit << 20)


def cost(flops, size):
    return pl.CostEstimate(flops=flops, bytes_accessed=size, transcendentals=0)


def in_vmem(value):
    return pltpu.with_memory_space_constraint(value, pltpu.VMEM)


def prefetch(own_t, other_t, own_s, other_s, after):
    (wide_t, columns), wide_s = own_t.shape, own_s.shape[0]
    return pl.pallas_call(
        prefetch_kernel,
        name="prefetch_heads",
        in_specs=[HBM] * 4 + [pl.BlockSpec(memory_space=pl.ANY)] * len(after),
        out_specs=[VMEM] * 2,
        out_shape=[pltpu.VMEM((wide_t, 2 * columns), BF16), pltpu.VMEM((wide_s, 2 * columns), BF16)],
        scratch_shapes=[pltpu.SemaphoreType.DMA((16,))],
        compiler_params=params(2),
        cost_estimate=cost(0, 8 * (wide_t + wide_s) * columns),
    )(*map(in_hbm, (own_t, other_t, own_s, other_s)), *after)


def logits_of(place, units, heads_t, heads_s):
    tokens = 8 * HALF
    (wide_t, columns), wide_s = heads_t.shape, heads_s.shape[0]
    logits = pltpu.VMEM((tokens, columns), F32)
    return pl.pallas_call(
        logits_kernel,
        name="logits",
        in_specs=[SMEM] + [HBM] * 8 + [VMEM] * 2,
        out_specs=[VMEM, VMEM, HBM, HBM],
        out_shape=[
            logits,
            logits,
            pltpu.HBM((64, 8, LANES), F32),
            pltpu.HBM((tokens, wide_s), BF16),
        ],
        scratch_shapes=[
            pltpu.VMEM((64, *units[0].shape[1:]), BF16),
            pltpu.VMEM((tokens, wide_t), BF16),
            pltpu.VMEM((tokens, wide_s), BF16),
            pltpu.VMEM((tokens, columns), F32),
            pltpu.VMEM((64, 8, LANES), F32),
            pltpu.VMEM((tokens, LANES), F32),
            pltpu.SemaphoreType.DMA((2, 8)),
            pltpu.SemaphoreType.DMA((2,)),
        ],
        compiler_params=params(24),
        cost_estimate=cost(2 * tokens * (wide_t + wide_s) * columns, 8 << 20),
    )(place, *map(in_hbm, units), *map(in_vmem, (heads_t, heads_s)))


def gradient_of(place, lengths, stats, teacher, student, own_s, other_s):
    tokens, columns = teacher.shape
    wide = own_s.shape[0]
    return pl.pallas_call(
        gradient_kernel,
        name="hidden_gradient",
        in_specs=[SMEM] * 2 + [VMEM] * 3 + [HBM] * 2,
        out_specs=[HBM, HBM, VMEM],
        out_shape=[
            pltpu.HBM((8, 8, HALF, wide // 8), BF16),
            pltpu.HBM((tokens, columns), BF16),
            jax.ShapeDtypeStruct((8, tokens), F32),
        ],
        scratch_shapes=[
            pltpu.VMEM((wide, columns), BF16),
            pltpu.VMEM((8, 8, HALF, wide // 8), BF16),
            pltpu.VMEM((tokens, columns), BF16),
            pltpu.VMEM((tokens, LANES), F32),
            pltpu.SemaphoreType.DMA((8,)),
            pltpu.SemaphoreType.DMA((5,)),
        ],
        compiler_params=params(LIMIT),
        cost_estimate=cost(2 * tokens * wide * columns, 2 * wide * columns),
    )(place, lengths, *map(in_vmem, (stats, teacher, student)), *map(in_hbm, (own_s, other_s)))


def head_gradient_of(own, other, mine, got):
    (tokens, wide), columns = own.shape, got.shape[1]
    width = wide // 8
    strip = pl.BlockSpec((tokens, width), lambda k: (0, k))
    whole = pl.BlockSpec((tokens, columns), lambda k: (0, 0))
    return pl.pallas_call(
        head_kernel,
        name="head_gradient",
        grid=(8,),
        in_specs=[strip, strip, whole, whole],
        out_specs=pl.BlockSpec((width, columns), lambda k: (k, 0)),
        out_shape=jax.ShapeDtypeStruct((wide, columns), BF16),
        compiler_params=params(LIMIT),
        cost_estimate=cost(4 * tokens * wide * columns, 16 << 20),
    )(own, other, mine, got)


def pack_kernel(core_ref, own_t_in, got_t, own_s_in, got_s, ids_ref, out_ref, own_t, own_s, sems):
    copies = [
        pltpu.make_async_copy(own_t_in, own_t, sems.at[0]),
        pltpu.make_async_copy(own_s_in, own_s, sems.at[1]),
    ]
    for copy in copies:
        copy.start()
    first = core_ref[0] == 0

    def sides(own_ref, got_ref):
        own, got = (ref[...].astype(F32) for ref in (own_ref, got_ref))
        own, got = (jnp.where(first, v[:HALF], v[HALF:]) for v in (own, got))
        return jnp.where(first, own, got), jnp.where(first, got, own)

    ids = jnp.where(first, ids_ref[:, :HALF], ids_ref[:, HALF:])
    ids = jnp.concatenate([ids, jnp.zeros((1, LANES - HALF), jnp.int32)], axis=1)
    ids = jnp.concatenate([ids // 4096, ids // 64 % 64, ids % 64, jnp.zeros((ID_ROWS - 3, LANES), jnp.int32)], axis=0)
    for copy in copies:
        copy.wait()
    teacher = jnp.concatenate(sides(own_t, got_t), axis=1)
    student = jnp.concatenate(sides(own_s, got_s), axis=1)
    rows = [teacher[:, i : i + LANES] for i in range(0, teacher.shape[1], LANES)]
    rows.append(ids.astype(F32))
    rows += [student[:, i : i + LANES] for i in range(0, student.shape[1], LANES)]
    block = jnp.concatenate(rows, axis=0).astype(BF16)
    out_ref[...] = jnp.broadcast_to(block, out_ref.shape)


def pack(core, own_t, got_t, own_s, got_s, sampled):
    rows = (own_t.shape[1] + own_s.shape[1]) * 2 * HALF // LANES + ID_ROWS
    return pl.pallas_call(
        pack_kernel,
        name="pack",
        in_specs=[SMEM, HBM, VMEM, HBM, VMEM, VMEM],
        out_specs=VMEM,
        out_shape=jax.ShapeDtypeStruct((8, rows, LANES), BF16),
        scratch_shapes=[
            pltpu.VMEM(own_t.shape, BF16),
            pltpu.VMEM(own_s.shape, BF16),
            pltpu.SemaphoreType.DMA((2,)),
        ],
        compiler_params=params(6),
        cost_estimate=cost(0, 1 << 20),
    )(core.reshape(1).astype(jnp.int32), in_hbm(own_t), in_vmem(got_t), in_hbm(own_s), in_vmem(got_s), sampled.reshape(1, 2 * HALF))


def per_device(teacher_hidden, student_hidden, teacher_head, student_head, lengths, sampled):
    group, member = lax.axis_index("grp"), lax.axis_index("vocab")
    core = member % 2
    is_first = core == 0
    wide_t, columns = teacher_head.shape
    wide_s = student_head.shape[0]
    tokens = 8 * HALF
    part_t, part_s = wide_t // 8, wide_s // 8
    strips_t, strips_s = part_t // LANES, part_s // LANES

    got_t, got_s = swap(teacher_hidden), swap(student_hidden)
    teacher_late, student_late, got_t, got_s = lax.optimization_barrier((teacher_head, student_head, got_t, got_s))
    other_teacher_head = swap(teacher_late)
    other_student_head = swap(student_late)

    blocks = pack(core, teacher_hidden, got_t, student_hidden, got_s, sampled)
    near = lax.all_to_all(blocks, BOTH, 0, 0, axis_index_groups=FIRST)
    near, other_student_head = lax.optimization_barrier((near, other_student_head))
    units = second_gather(near)
    heads_t, heads_s = prefetch(
        teacher_head, other_teacher_head, student_head, other_student_head, units[1:4]
    )

    number_of = group * lax.axis_size("vocab") + member
    x_high, y, x_low, z = member // 8, member // 2 % 4, group // 4, group % 4
    corner = x_high * 4 + y // 2 * 2 + z // 2
    corner = corner ^ (core * (x_low * 4 + y % 2 * 2 + z % 2))
    place = [number_of * columns, (number_of + 1 - 2 * core) * columns, corner, core]
    place = jnp.stack(place).astype(jnp.int32)
    teacher_logits, student_logits, stats, own_rows = logits_of(place, units, heads_t, heads_s)
    all_stats = lax.all_to_all(stats, BOTH, 0, 0, axis_index_groups=SAME_CORE)

    part, grads, kl = gradient_of(
        place, lengths, all_stats, teacher_logits, student_logits, student_head, other_student_head
    )
    grads, late_rows = lax.optimization_barrier((grads, own_rows))
    other_rows = swap(late_rows)
    got_grad = swap(grads[:, columns:])

    def spread(value, groups):
        return lax.all_to_all(value, BOTH, 0, 0, axis_index_groups=groups)

    parts = spread(part, SECOND)
    head_grad = head_gradient_of(own_rows, other_rows, grads, got_grad)
    parts, head_grad = lax.optimization_barrier((parts, head_grad))
    parts = spread(jnp.sum(parts.astype(F32), axis=0).astype(BF16), FIRST)
    hidden = jnp.sum(parts.astype(F32), axis=0).astype(BF16)
    one, two = hidden[:, : part_s // 2], hidden[:, part_s // 2 :]
    kept = jnp.where(is_first, one, two)
    got = swap(jnp.where(is_first, two, one))
    hidden_grad = jnp.concatenate(
        [jnp.where(is_first, kept, got), jnp.where(is_first, got, kept)], axis=0
    )

    def own_tokens(who):
        return lax.dynamic_slice(kl, (0, group * HALF + (4 * who) % HALF), (2, 4))

    got = swap(own_tokens(member + 1 - 2 * core))
    out = jnp.where(member // 8 == core, own_tokens(member), got)
    return head_grad, hidden_grad, out[0], out[1]


def solution(mesh):
    return jax.shard_map(
        per_device,
        mesh=mesh,
        in_specs=(
            P("grp", "vocab"),
            P("grp", "vocab"),
            P(None, BOTH),
            P(None, BOTH),
            P(),
            P("grp"),
        ),
        out_specs=(P(None, BOTH), P("grp", "vocab"), P(BOTH), P(BOTH)),
        check_vma=False,
    )
```
